32 devices in a mesh: row: 4 (over y, x), col: 8 (over z, core).
Axes of the slice: x: 2, y: 2, z: 4, core: 2. Of those that a mesh axis runs over, the one named last changes fastest.
Arguments:
- cooc: int32 [8192, 16384], P('row', 'col'), may hold values from 0 to 48
- tile_list: int32 [4, 8, 4], P('row', 'col'), may hold values from -1 to 3, as said below
- marginal: int32 [16384], P(('col', 'row')), may hold values from 8 to 524287
- embed: float32 [16384, 256], P(('col', 'row')), may hold values from -1.5 to 1.5
- accum: float32 [16384, 256], P(('col', 'row')), may hold values from 0.001 to 0.01
Outputs:
- new_embed: float32 [16384, 256], P(('col', 'row'))
- new_accum: float32 [16384, 256], P(('col', 'row'))
The draws below stay inside these ranges and needn't reach their ends.
Inputs may be any that keep to these rules, and one draw needn't show every extreme that they name: `tile_list`: the first entries of each device's list are distinct local tile numbers, the rest are -1; every device lists at least one tile and some device lists all 4.
All inputs are finite; a program needn't handle non-finite values.
Results may differ from the reference program's by a relative error of at most 0.0003.
Values sent between devices are 32-bit elements; how exact they have to be, the bound alone decides.
No kernel may reach another device: no remote copies, remote signals or barrier semaphores. Data moves between devices by JAX's collectives and lax.ppermute only.
A program may use at most 128 MiB of HBM per device.

```python
import math
import jax
import jax.numpy as jnp
from jax import lax

D = 256
BLOCK = 1024
RB = 2
CB = 2
ROWGROUPS = 4
COLGROUPS = 8
TILES_DEV = 4
SLAB_ROWS = 8192
VOCAB = 16384


def draw_cooc(key, part):
    key = jax.random.fold_in(key, 11)
    drawn = jax.random.randint(key, (SLAB_ROWS, VOCAB), 0, 96, dtype=jnp.int32)
    return jnp.maximum(drawn - 47, 0).astype(jnp.int32)


def draw_tile_list(key, part):
    key = jax.random.fold_in(key, 5)
    first, second, third, fourth = jax.random.split(key, 4)
    devices = ROWGROUPS * COLGROUPS
    scores_int = jax.random.randint(first, (devices, TILES_DEV), 0, 1 << 20, dtype=jnp.int32) * TILES_DEV + jnp.arange(TILES_DEV, dtype=jnp.int32)[None, :]
    ordering = jnp.argsort(scores_int, axis=1, stable=True).astype(jnp.int32)
    light = jax.random.randint(second, (devices,), 0, 8, dtype=jnp.int32) < 5
    listed = jnp.where(light, 1, jax.random.randint(third, (devices,), 1, TILES_DEV + 1, dtype=jnp.int32))
    fullest = jax.random.randint(fourth, (), 0, devices, dtype=jnp.int32)
    listed = jnp.where(jnp.arange(devices, dtype=jnp.int32) == fullest, TILES_DEV, listed)
    position = jnp.arange(TILES_DEV, dtype=jnp.int32)[None, :]
    chosen = jnp.where(position < listed[:, None], ordering, -1)
    return chosen.reshape(ROWGROUPS, COLGROUPS, TILES_DEV).astype(jnp.int32)


def draw_marginal(key, part):
    key = jax.random.fold_in(key, 7)
    first, second, third, fourth = jax.random.split(key, 4)
    items = jnp.arange(VOCAB, dtype=jnp.int32)
    exponent = jax.random.randint(first, (VOCAB,), 3, 18, dtype=jnp.int32) + 2 * items // VOCAB
    lowest = jnp.left_shift(jnp.ones((VOCAB,), jnp.int32), exponent)
    extra = jax.random.randint(second, (VOCAB,), 0, lowest, dtype=jnp.int32)
    values = lowest + extra
    low_item = jax.random.randint(third, (), 0, VOCAB, dtype=jnp.int32)
    high_item = (low_item + 1 + jax.random.randint(fourth, (), 0, VOCAB - 1, dtype=jnp.int32)) % VOCAB
    values = jnp.where(items == low_item, 8, values)
    values = jnp.where(items == high_item, 524287, values)
    return values.astype(jnp.int32)


def level_of(rng, dims, cuts, low, largest):
    def one(dim, shards_of):
        heights = jax.random.uniform(jax.random.fold_in(jax.random.fold_in(rng, 6), dim), (shards_of,), jnp.float32, low / len(cuts), largest / len(cuts))
        return jnp.repeat(jnp.exp(heights), dims[dim] // shards_of).reshape((-1,) + (1,) * (len(dims) - dim - 1))

    level = one(*cuts[0])
    for cut in cuts[1:]:
        level = level * one(*cut)
    return level


def bell_draw(own_key, dims, scale, reach, pieces=(), kind=jnp.bfloat16):
    values = jax.random.normal(own_key, dims, jnp.float32) * scale
    if len(pieces) > 0:
        values = level_of(own_key, dims, pieces, -0.22, 0.18) * values
    return jnp.clip(values, min=-reach, max=reach).astype(kind)


def setup_inputs(seed: int = 0) -> dict:
    key_of = jax.random.split(jax.random.key(seed), 6)
    return {
        "cooc": draw_cooc(jax.random.fold_in(key_of[5], 71), 0),
        "tile_list": draw_tile_list(jax.random.fold_in(key_of[5], 71), 0),
        "marginal": draw_marginal(jax.random.fold_in(key_of[5], 71), 0),
        "embed": bell_draw(key_of[3], (VOCAB, D), 0.25, 1.5, ((0, 32),), jnp.float32),
        "accum": jnp.clip(jnp.exp(math.log(0.01) - 2.30258502 * jax.random.uniform(key_of[4], (VOCAB, D), jnp.float32) ** level_of(key_of[4], (VOCAB, D), ((0, 32),), -0.2, 0.2)), 0.001, 0.01),
    }


LEARN_RATE = 0.05

def tile_grads(counts, row_vecs, col_vecs, row_logs, col_logs, log_total):
    scores = lax.dot_general(row_vecs, col_vecs, (((1,), (1,)), ((), ())), precision=lax.Precision.HIGHEST, preferred_element_type=jnp.float32)
    centred = scores + row_logs[:, None] + col_logs[None, :] - log_total
    counts_f = counts.astype(jnp.float32)
    weights = 0.1 + 0.25 * jnp.sqrt(counts_f)
    slopes = jnp.where(counts > 0, weights * (centred - jnp.log(jnp.maximum(counts_f, 1.0))), jax.nn.sigmoid(centred))
    to_rows = jnp.dot(slopes, col_vecs, precision=lax.Precision.HIGHEST, preferred_element_type=jnp.float32)
    to_cols = lax.dot_general(slopes, row_vecs, (((0,), (0,)), ((), ())), precision=lax.Precision.HIGHEST, preferred_element_type=jnp.float32)
    return (to_rows, to_cols)

def reference(cooc, tile_list, marginal, embed, accum):
    marg_f = marginal.astype(jnp.float32)
    log_marg = jnp.log(marg_f)
    log_total = jnp.log(jnp.sum(marg_f))
    flat_list = tile_list.reshape(-1)

    def visit(gradients, flat_index):
        entry = flat_list[flat_index]
        group = flat_index // TILES_DEV
        row_group = group // COLGROUPS
        col_group = group % COLGROUPS
        tile_local = jnp.maximum(entry, 0)
        row_start = ((row_group * RB + tile_local // CB) * BLOCK).astype(jnp.int32)
        col_start = ((col_group * CB + tile_local % CB) * BLOCK).astype(jnp.int32)

        def with_tile(current):
            counts = lax.dynamic_slice(cooc, (row_start, col_start), (BLOCK, BLOCK))
            row_vecs = lax.dynamic_slice_in_dim(embed, row_start, BLOCK, 0)
            col_vecs = lax.dynamic_slice_in_dim(embed, col_start, BLOCK, 0)
            row_logs = lax.dynamic_slice_in_dim(log_marg, row_start, BLOCK, 0)
            col_logs = lax.dynamic_slice_in_dim(log_marg, col_start, BLOCK, 0)
            to_rows, to_cols = tile_grads(counts, row_vecs, col_vecs, row_logs, col_logs, log_total)
            current = lax.dynamic_update_slice_in_dim(current, lax.dynamic_slice_in_dim(current, row_start, BLOCK, 0) + to_rows, row_start, 0)
            current = lax.dynamic_update_slice_in_dim(current, lax.dynamic_slice_in_dim(current, col_start, BLOCK, 0) + to_cols, col_start, 0)
            return current

        def unchanged(current):
            return current
        return (lax.cond(entry >= 0, with_tile, unchanged, gradients), None)
    start = jnp.zeros(embed.shape, jnp.float32)
    gradients, _ = lax.scan(visit, start, jnp.arange(ROWGROUPS * COLGROUPS * TILES_DEV, dtype=jnp.int32))
    gradients = gradients / BLOCK
    new_accum = accum + gradients * gradients
    new_embed = embed - LEARN_RATE * gradients / jnp.sqrt(new_accum)
    return (new_embed, new_accum)
```

```python
import functools

import jax
import jax.numpy as jnp
from jax import lax
from jax.experimental import pallas as pl
from jax.experimental.pallas import tpu as pltpu
from jax.sharding import PartitionSpec as P

BLOCK = 1024
LEARN_RATE = 0.05
SUB = 256
PAD = 8


def split_bf16(values):
    high = values.astype(jnp.bfloat16)
    low = (values - high.astype(jnp.float32)).astype(jnp.bfloat16)
    return high, low


def product(left, right, dims):
    (left_at,), (right_at,) = dims
    left = jnp.concatenate([left[0], left[1], left[0]], axis=left_at)
    right = jnp.concatenate([right[0], right[0], right[1]], axis=right_at)
    return lax.dot_general(left, right, (dims, ((), ())), preferred_element_type=jnp.float32)


def shard_kernel(m, groups, share, layout, first, last, extra, *refs):
    rest = list(refs)
    take = lambda count: [rest.pop(0) for _ in range(count)]
    place_ref, listed_ref, total_ref, here_ref, there_ref, cooc_ref = take(6)
    if first:
        pieces = take(len(layout))
    else:
        high_ref, low_ref, log_ref, sums_in = take(4)
    take(extra)
    mine_out, other_out = take(2)
    if first:
        high_ref, low_ref, log_ref = take(3)
    if last:
        outs = take(2 * groups)
    else:
        (sums,) = take(1)
    row_vecs, row_out, cells, row_sem, cell_sems = take(5)
    if last:
        (sums,) = take(1)

    cols = groups * share
    col_blocks = cols // BLOCK
    per = share // SUB
    g = place_ref[0]
    here = place_ref[1]
    shard = g ^ m
    row_block = shard * share // BLOCK

    def cell_copy(block):
        return pltpu.make_async_copy(
            cooc_ref.at[pl.ds(pl.multiple_of(shard * share, share), share), pl.ds(block * BLOCK, BLOCK)],
            cells.at[block],
            cell_sems.at[block],
        )

    def is_listed(block):
        return listed_ref[row_block * col_blocks + block] > 0

    for block in range(col_blocks):

        @pl.when(is_listed(block))
        def _():
            cell_copy(block).start()

    @pl.when(here > 0)
    def _():
        copy = pltpu.make_async_copy(here_ref, row_vecs, row_sem)
        copy.start()
        copy.wait()

    @pl.when(here == 0)
    def _():
        copy = pltpu.make_async_copy(there_ref, row_vecs, row_sem)
        copy.start()
        copy.wait()

    if first:
        for piece, (other, start, count) in zip(pieces, layout):
            body = min(count, share - start)
            at = pl.multiple_of((g ^ other) * share + start, PAD)
            high, low = split_bf16(piece[:body, :])
            high_ref[pl.ds(at, body), :] = high
            low_ref[pl.ds(at, body), :] = low
            if body < count:
                at = pl.multiple_of((g ^ other) * PAD, PAD)
                log_ref[pl.ds(at, PAD), :] = piece[body:, :]

    row_log = [
        jnp.transpose(jnp.broadcast_to(row_vecs[share + k : share + k + 1, :], (128, SUB))) for k in range(per)
    ]
    row_log = jnp.concatenate(row_log, axis=0) - total_ref[0]
    row_log = jnp.concatenate([row_log] * (SUB // 128), axis=1)
    rows = row_vecs[:share, :]
    row_pair = split_bf16(rows)
    row_turned = split_bf16(jnp.transpose(rows))
    row_out[...] = jnp.zeros_like(row_out)

    for block in range(col_blocks):
        span = slice(block * BLOCK, (block + 1) * BLOCK)

        @pl.when(is_listed(block))
        def _():
            cell_copy(block).wait()
            strips = BLOCK // SUB

            def col_pair(strip):
                at = block * BLOCK + strip * SUB
                return high_ref[at : at + SUB, :], low_ref[at : at + SUB, :]

            def scores(strip):
                return product(row_pair, col_pair(strip), ((1,), (1,)))

            def slopes(strip, values):
                at = block * BLOCK + strip * SUB
                log_at = at // share * PAD + at % share // SUB
                centred = values + row_log + log_ref[log_at : log_at + 1, :]
                counts_f = cells[block, :, strip * SUB : (strip + 1) * SUB].astype(jnp.float32)
                floor = jnp.maximum(counts_f, 1.0)
                weights = 0.1 + 0.25 * (counts_f * lax.rsqrt(floor))
                return split_bf16(
                    jnp.where(
                        counts_f > 0,
                        weights * (centred - jnp.log(floor)),
                        0.5 * jnp.tanh(0.5 * centred) + 0.5,
                    )
                )

            def gradients(strip, pair):
                at = block * BLOCK + strip * SUB
                row_out[...] += product(pair, col_pair(strip), ((1,), (0,)))
                added = product(row_turned, pair, ((1,), (0,)))
                if not first:
                    added = added + sums_in[:, at : at + SUB]
                sums[:, at : at + SUB] = added

            ahead = scores(0)
            behind = None
            for strip in range(strips):
                values = ahead
                if strip + 1 < strips:
                    ahead = scores(strip + 1)
                if strip > 0:
                    gradients(strip - 1, behind)
                behind = slopes(strip, values)
            gradients(strips - 1, behind)

        @pl.when(jnp.logical_not(is_listed(block)))
        def _():
            if first:
                sums[:, span] = jnp.zeros((sums.shape[0], BLOCK), jnp.float32)
            else:
                sums[:, span] = sums_in[:, span]

    half = share // 2
    core = place_ref[2]
    mine_out[...] = row_out[pl.ds(pl.multiple_of(core * half, half), half), :]
    other_out[...] = row_out[pl.ds(pl.multiple_of((1 - core) * half, half), half), :]
    if last:
        for other in range(groups):
            at = pl.multiple_of((g ^ other) * share, share)
            block = jnp.transpose(sums[:, pl.ds(at, share)])
            outs[2 * other][...] = block[:half]
            outs[2 * other + 1][...] = block[half:]


def shard_grads(m, groups, share, layout, place, listed, total, here, there, cooc, held, sums, ready, last):
    depth = here.shape[1]
    cols = groups * share
    first = m == 0
    whole = pl.BlockSpec(memory_space=pltpu.VMEM)
    scalar = pl.BlockSpec(memory_space=pltpu.SMEM)
    remote = pl.BlockSpec(memory_space=pl.ANY)
    vec = jax.ShapeDtypeStruct((share // 2, depth), jnp.float32)
    turned = jax.ShapeDtypeStruct((depth, cols), jnp.float32)
    coded = jax.ShapeDtypeStruct((cols, depth), jnp.bfloat16)
    logs = jax.ShapeDtypeStruct((groups * PAD, depth), jnp.float32)
    out_shape = [vec, vec]
    if first:
        out_shape += [coded, coded, logs]
    if last:
        out_shape += [vec] * (2 * groups)
    else:
        out_shape += [turned]
    args = [place, listed, total, here, there, cooc, *held] + ([] if first else [sums])
    in_specs = [scalar] * 3 + [remote] * 3 + [whole] * (len(args) - 6)
    args += ready
    in_specs += [remote] * len(ready)
    scratch = [
        pltpu.VMEM(here.shape, jnp.float32),
        pltpu.VMEM((share, depth), jnp.float32),
        pltpu.VMEM((cols // BLOCK, share, BLOCK), jnp.int32),
        pltpu.SemaphoreType.DMA,
        pltpu.SemaphoreType.DMA((cols // BLOCK,)),
    ]
    if last:
        scratch.append(pltpu.VMEM((depth, cols), jnp.float32))
    cells = share * cols
    return pl.pallas_call(
        functools.partial(shard_kernel, m, groups, share, layout, first, last, len(ready)),
        out_shape=out_shape,
        in_specs=in_specs,
        out_specs=[whole] * len(out_shape),
        scratch_shapes=scratch,
        compiler_params=pltpu.CompilerParams(vmem_limit_bytes=42 * 2**20),
        cost_estimate=pl.CostEstimate(
            flops=cells * depth * 18, bytes_accessed=4 * cells + 8 * cols * depth, transcendentals=3 * cells
        ),
        name="shard_grads",
    )(*args)


def closed(pairs, count):
    target = dict(pairs)
    sources = {t: f for f, t in pairs}
    for start in range(0, count, 2):
        if not any(device in target or device in sources for device in (start, start + 1)):
            target[start], target[start + 1] = start + 1, start
            sources[start], sources[start + 1] = start + 1, start
    for start in range(count):
        if start not in sources:
            end = start
            while end in target:
                end = target[end]
            target[end] = start
    return sorted(target.items())


def local(groups, col_groups, cooc, tile_list, marginal, embed, accum):
    chips = col_groups // 2
    mid = (groups - 1) // 2
    both = ("row", "col")
    g = lax.axis_index("row")
    h = lax.axis_index("col")
    chip = h // 2
    core = h % 2
    root_chip = g // 2
    share, depth = embed.shape
    half = share // 2
    rows = range(groups)

    def ident(row, at, core):
        return row * col_groups + at * 2 + core

    def permute(value, pairs):
        return lax.ppermute(value, both, closed(pairs, groups * col_groups))

    def swapped(value, axis, m, size):
        return lax.ppermute(value, axis, [(r, r ^ m) for r in range(size)])

    def row_swapped(value, m):
        return swapped(value, "row", m, groups)

    def across(value):
        return swapped(value, "col", 1, col_groups)

    marg_f = marginal.astype(jnp.float32)
    logs = jnp.log(marg_f).reshape(share // depth, depth)
    coded = jnp.concatenate([embed, jnp.pad(logs, ((0, PAD - share // depth), (0, 0)))], axis=0)
    split = (share + PAD) // 2 // PAD * PAD
    pieces = {0: [coded]}
    layout = [(0, 0, share + PAD)]
    for m in range(1, groups):
        low = m & -m
        if low == m:
            pieces[m] = [row_swapped(coded, m)]
            layout.append((m, 0, share + PAD))
    for m in range(1, groups):
        low = m & -m
        if low != m:
            high = 1 << (m.bit_length() - 1)
            one = jnp.concatenate(pieces[m ^ low], axis=0)[:split]
            two = jnp.concatenate(pieces[m ^ high], axis=0)[split:]
            pieces[m] = [row_swapped(one, low), row_swapped(two, high)]
            layout += [(m, 0, split), (m, split, share + PAD - split)]
    held = [pieces[m][start > 0] for m, start, _ in layout]

    if groups == 4 and chips == 4:
        heres, events = rows_by_line(coded, split, g, chip, ident, permute, lambda value, pairs: lax.ppermute(value, both, pairs))
    else:
        heres, events = rows_by_chain(pieces, rows, chips, root_chip, chip, ident, permute), []

    total = jnp.broadcast_to(jnp.sum(marg_f), (8, 128))
    steps = [("col", 1 << k, col_groups) for k in range(col_groups.bit_length() - 1)]
    steps += [("row", 1 << k, groups) for k in range(groups.bit_length() - 1)]
    top_row = lax.broadcasted_iota(jnp.int32, (8, 128), 0) == 0
    for axis, step, size in steps:
        if events:
            total = jnp.where(top_row, total, events.pop(0))
        total = total + swapped(total, axis, step, size)
    total = jnp.log(total[0, :1])
    theres = [across(here) for here in heres]

    meet = [([], []) for _ in range(max(chips - 1 - mid, mid))]
    for step in range(chips - 1 - mid):
        meet[step][1].append(chips - 2 - step)
        meet[step][0].extend((ident(r, chips - 1 - step, c), ident(r, chips - 2 - step, c)) for r in rows for c in (0, 1))
    for step in range(mid):
        meet[step][1].append(step + 1)
        meet[step][0].extend((ident(r, step, c), ident(r, step + 1, c)) for r in rows for c in (0, 1))

    listing = tile_list.reshape(-1)
    listed = jnp.sum((listing[None, :] == jnp.arange(listing.shape[0])[:, None]).astype(jnp.int32), axis=1)
    place = jnp.stack([g, (core == g % 2).astype(jnp.int32), core]).astype(jnp.int32)

    stages = []
    sums = None
    for m in rows:
        last = m == groups - 1
        ready = []
        if m >= 2:
            ready.append(stages[m - 2][0])
        if m >= 3:
            ready.append(stages[m - 3][1])
        outs = shard_grads(
            m, groups, share, layout, place, listed, total, heres[m], theres[m], cooc, held, sums, ready, last
        )
        part = outs[0] + across(outs[1])
        if m == 0:
            held = outs[2:5]
        sums = outs[-1]
        hops = [part]
        for pairs, targets in meet:
            taking = functools.reduce(jnp.logical_or, [chip == target for target in targets])
            part = jnp.where(taking, part + permute(part, pairs), part)
            hops.append(part)
        stages.append(hops)

    halves = outs[2:]
    if groups == 4:
        first_x = row_swapped(jnp.concatenate([halves[2], halves[6]], axis=0), 1)
        first_y = row_swapped(jnp.concatenate([halves[5], halves[7]], axis=0), 2)
        stages[-1][-1] = jnp.where(chip == mid, part, jnp.where(core == 0, first_x[:half], first_y[:half]))
        second_x = row_swapped(halves[3] + first_y[half:], 1)
        second_y = row_swapped(halves[4] + first_x[half:], 2)
        top = halves[0] + first_x[:half] + second_y
        bottom = halves[1] + second_x + first_y[:half]
    else:
        top, bottom = halves[:2]
        for m in range(1, groups):
            top = top + row_swapped(halves[2 * m], m)
            bottom = bottom + row_swapped(halves[2 * m + 1], m)

    mine = other = jnp.zeros_like(part)
    for m in rows:
        home = [(ident(r, mid, c), ident(r ^ m, r // 2, c)) for r in rows for c in (0, 1)]
        arrived = permute(stages[m][-1], home)
        mine = jnp.where(h == g ^ m, arrived, mine)
        other = jnp.where(h ^ 1 == g ^ m, arrived, other)
    theirs = across(other)
    row_top = jnp.where(core == 0, mine, theirs)
    row_bottom = jnp.where(core == 0, theirs, mine)
    gradients = jnp.concatenate([top + row_top, bottom + row_bottom], axis=0) / BLOCK
    new_accum = accum + gradients * gradients
    new_embed = embed - LEARN_RATE * gradients / jnp.sqrt(new_accum)
    return (new_embed, new_accum)


def rows_by_line(coded, split, g, chip, ident, permute, permute_some):
    rows = range(4)

    def line(value, chain):
        return permute(value, [(ident(r, a, c), ident(r, b, c)) for r in rows for c in (0, 1) for a, b in chain])

    near, far, events = [], [], []
    down = line(coded, [(1, 0)])
    for part, back in ((coded[:split], down[:split]), (coded[split:], down[split:])):
        one = line(part, [(0, 1), (1, 2)])
        two = line(one, [(1, 2), (2, 3)])
        three = line(two, [(2, 3)])
        events.append((one, two, three))
        from_zero = jnp.where(chip == 0, part, jnp.where(chip == 1, one, jnp.where(chip == 2, two, three)))
        from_one = jnp.where(chip == 0, back, jnp.where(chip == 1, part, jnp.where(chip == 2, one, two)))
        near.append(jnp.where(g < 2, from_zero, from_one))
        far.append(jnp.where(g < 2, from_one, from_zero))
    near = jnp.concatenate(near, axis=0)
    far = jnp.concatenate(far, axis=0)

    def plane(value, m):
        return permute_some(value, [(ident(r ^ m, at, r % 2), ident(r, at, r % 2)) for r in rows for at in rows])

    events = [events[0][0], events[1][0], events[0][1], events[1][1], events[0][2]]
    return [near, plane(near, 1), plane(far, 2), plane(far, 3)], [event[:8, :128] for event in events]


def rows_by_chain(pieces, rows, chips, root_chip, chip, ident, permute):
    heres = []
    for m in rows:
        own = jnp.concatenate(pieces[m], axis=0)
        here = own
        for sign in (1, -1):
            hop = own
            for d in range(1, chips):
                pairs = [
                    (ident(r, r // 2 + sign * (d - 1), r % 2), ident(r, r // 2 + sign * d, r % 2))
                    for r in rows
                    if 0 <= r // 2 + sign * d < chips
                ]
                if pairs:
                    hop = permute(hop, pairs)
                    here = jnp.where(chip == root_chip + sign * d, hop, here)
        heres.append(here)
    return heres


def solution(mesh):
    placed = (
        P("row", "col"),
        P("row", "col", None),
        P(("col", "row")),
        P(("col", "row"), None),
        P(("col", "row"), None),
    )
    return jax.shard_map(
        functools.partial(local, mesh.shape["row"], mesh.shape["col"]),
        mesh=mesh,
        in_specs=placed,
        out_specs=(P(("col", "row"), None), P(("col", "row"), None)),
        check_vma=False,
    )
```

```python
import functools

import jax
import jax.numpy as jnp
from jax import lax
from jax.experimental import pallas as pl
from jax.experimental.pallas import tpu as pltpu
from jax.sharding import PartitionSpec as P

BLOCK = 1024
LEARN_RATE = 0.05
SUB = 512
PAD = 8
VMEM_LIMIT = 42 * 2**20


def split_bf16(values):
    high = values.astype(jnp.bfloat16)
    low = (values - high.astype(jnp.float32)).astype(jnp.bfloat16)
    return high, low


def product(left, right, dims):
    (left_at,), (right_at,) = dims
    left = jnp.concatenate([left[0], left[1], left[0]], axis=left_at)
    right = jnp.concatenate([right[0], right[0], right[1]], axis=right_at)
    return lax.dot_general(left, right, (dims, ((), ())), preferred_element_type=jnp.float32)


def half_kernel(k, groups, share, layout, tiles, first, added, ends, last, extra, *refs):
    rest = list(refs)
    take = lambda count: [rest.pop(0) for _ in range(count)]
    place_ref, listed_ref, cooc_ref, mine_ref, theirs_ref = take(5)
    if first:
        pieces = take(len(layout))
    else:
        high_ref, low_ref, log_ref, sums_in = take(4)
    if added:
        (row_in,) = take(1)
    take(extra)
    if ends:
        mine_out, other_out = take(2)
    else:
        (row_out,) = take(1)
    if first:
        high_ref, low_ref, log_ref = take(3)
    if last:
        outs = take(2 * groups)
    else:
        (sums,) = take(1)
    row_vecs, row_logs, cells, cell_sems = take(4)
    if ends:
        (row_out,) = take(1)
    if last:
        (sums,) = take(1)

    depth = row_vecs.shape[1]
    half = share // 2
    quarter = share // 4
    cols = groups * share
    col_blocks = cols // BLOCK
    per = BLOCK // share
    tall = BLOCK // 2
    g = place_ref[0]
    chip = place_ref[1]
    core = place_ref[2]

    def cell_copies(row, col):
        number = tiles.index((row, col))
        return [
            pltpu.make_async_copy(
                cooc_ref.at[pl.ds((row * per + j) * share + k * half, half), pl.ds(col * BLOCK, BLOCK)],
                cells.at[number, pl.ds(j * half, half), :],
                cell_sems.at[number, j],
            )
            for j in range(per)
        ]

    for row, col in tiles:

        @pl.when(listed_ref[row * col_blocks + col] > 0)
        def _():
            for copy in cell_copies(row, col):
                copy.start()

    if first:
        total = jnp.zeros((1, 128), jnp.float32)
        for ref in (mine_ref, theirs_ref):
            for d in range(groups):
                at = d * (quarter + PAD) + quarter + 1
                total = total + ref[at : at + 1, :128]
        log_total = jnp.concatenate([jnp.log(total)] * (depth // 128), axis=1)
        for piece, (other, start, count) in zip(pieces, layout):
            body = min(count, share - start)
            at = pl.multiple_of((g ^ other) * share + start, 16)
            high, low = split_bf16(piece[:body, :])
            high_ref[pl.ds(at, body), :] = high
            low_ref[pl.ds(at, body), :] = low
            if body < count:
                at = pl.multiple_of((g ^ other) * PAD, PAD)
                log_ref[pl.ds(at, PAD), :] = piece[body:, :] - log_total
        sums[...] = jnp.zeros_like(sums)
    else:
        sums[...] = sums_in[...]

    for ref, side in ((mine_ref, core), (theirs_ref, 1 - core)):
        for d in range(groups):
            start = d * (quarter + PAD)
            at = pl.multiple_of((chip ^ d) * half + side * quarter, quarter)
            row_vecs[pl.ds(at, quarter), :] = ref[start : start + quarter, :]
            log_row = ref[start + quarter : start + quarter + 1, :128]
            row_logs[pl.ds(at, quarter), :] = jnp.transpose(jnp.broadcast_to(log_row, (128, 128)))[:quarter, :]
    row_out[...] = row_in[...] if added else jnp.zeros_like(row_out)

    for row, col in tiles:
        tall_rows = slice(row * tall, (row + 1) * tall)

        @pl.when(listed_ref[row * col_blocks + col] > 0)
        def _():
            for copy in cell_copies(row, col):
                copy.wait()
            rows = row_vecs[tall_rows, :]
            row_pair = split_bf16(rows)
            row_turned = split_bf16(jnp.transpose(rows))
            row_log = jnp.concatenate([row_logs[tall_rows, :]] * (SUB // 128), axis=1)
            strips = BLOCK // SUB

            def col_pair(strip):
                at = col * BLOCK + strip * SUB
                return high_ref[at : at + SUB, :], low_ref[at : at + SUB, :]

            def scores(strip):
                return product(row_pair, col_pair(strip), ((1,), (1,)))

            def slopes(strip, values):
                at = col * BLOCK + strip * SUB
                log_rows = [lane // share * PAD + lane % share // depth for lane in range(at, at + SUB, depth)]
                col_log = jnp.concatenate([log_ref[q : q + 1, :] for q in log_rows], axis=1)
                centred = values + row_log + col_log
                counts = cells[tiles.index((row, col)), :, strip * SUB : (strip + 1) * SUB]
                counts_f = counts.astype(jnp.float32)
                floor = jnp.maximum(counts_f, 1.0)
                weights = 0.1 + 0.25 * (counts_f * lax.rsqrt(floor))
                return split_bf16(
                    jnp.where(
                        counts_f > 0,
                        weights * (centred - jnp.log(floor)),
                        0.5 * jnp.tanh(0.5 * centred) + 0.5,
                    )
                )

            def gradients(strip, pair):
                at = col * BLOCK + strip * SUB
                row_out[tall_rows, :] += product(pair, col_pair(strip), ((1,), (0,)))
                sums[:, at : at + SUB] += product(row_turned, pair, ((1,), (0,)))

            ahead = scores(0)
            behind = None
            for strip in range(strips):
                values = ahead
                if strip + 1 < strips:
                    ahead = scores(strip + 1)
                if strip > 0:
                    gradients(strip - 1, behind)
                behind = slopes(strip, values)
            gradients(strips - 1, behind)

    for out, side in ((mine_out, core), (other_out, 1 - core)) if ends else ():
        for d in range(groups):
            at = pl.multiple_of((chip ^ d) * half + side * quarter, quarter)
            out[d * quarter : (d + 1) * quarter, :] = row_out[pl.ds(at, quarter), :]
    if last:
        for other in range(groups):
            at = pl.multiple_of((g ^ other) * share, share)
            block = jnp.transpose(sums[:, pl.ds(at, share)])
            outs[2 * other][...] = block[:half]
            outs[2 * other + 1][...] = block[half:]


def half_grads(k, groups, share, layout, tiles, place, listed, cooc, mine, theirs, held, row_in, ready):
    depth = mine.shape[1]
    cols = groups * share
    first = k == 0
    added = row_in is not None
    ends = tiles[-1] == (cols // BLOCK - 1,) * 2
    last = ends and k == 1
    per = BLOCK // share
    rows = groups * share // 2
    whole = pl.BlockSpec(memory_space=pltpu.VMEM)
    scalar = pl.BlockSpec(memory_space=pltpu.SMEM)
    remote = pl.BlockSpec(memory_space=pl.ANY)
    row_part = jax.ShapeDtypeStruct((rows // 2, depth), jnp.float32)
    row_all = jax.ShapeDtypeStruct((rows, depth), jnp.float32)
    col_half = jax.ShapeDtypeStruct((share // 2, depth), jnp.float32)
    coded = jax.ShapeDtypeStruct((cols, depth), jnp.bfloat16)
    logs = jax.ShapeDtypeStruct((groups * PAD, depth), jnp.float32)
    turned = jax.ShapeDtypeStruct((depth, cols), jnp.float32)
    out_shape = [row_part] * 2 if ends else [row_all]
    out_shape += [coded, coded, logs] if first else []
    out_shape += [col_half] * (2 * groups) if last else [turned]
    held = [*held, row_in] if added else [*held]
    args = [place, listed, cooc, mine, theirs, *held, *ready]
    in_specs = [scalar] * 2 + [remote] + [whole] * (2 + len(held)) + [remote] * len(ready)
    scratch = [
        pltpu.VMEM((rows, depth), jnp.float32),
        pltpu.VMEM((rows, 128), jnp.float32),
        pltpu.VMEM((len(tiles), BLOCK // 2, BLOCK), jnp.int32),
        pltpu.SemaphoreType.DMA((len(tiles), per)),
    ]
    if ends:
        scratch.append(pltpu.VMEM((rows, depth), jnp.float32))
    if last:
        scratch.append(pltpu.VMEM((depth, cols), jnp.float32))
    cells = len(tiles) * BLOCK * BLOCK // 2
    return pl.pallas_call(
        functools.partial(half_kernel, k, groups, share, layout, tiles, first, added, ends, last, len(ready)),
        out_shape=out_shape,
        in_specs=in_specs,
        out_specs=[whole] * len(out_shape),
        scratch_shapes=scratch,
        compiler_params=pltpu.CompilerParams(vmem_limit_bytes=VMEM_LIMIT),
        cost_estimate=pl.CostEstimate(
            flops=cells * depth * 18, bytes_accessed=4 * cells + 8 * cols * depth, transcendentals=3 * cells
        ),
        name="half_grads",
    )(*args)


def local(groups, col_groups, cooc, tile_list, marginal, embed, accum):
    assert col_groups == 2 * groups and groups & (groups - 1) == 0
    both = ("row", "col")
    g = lax.axis_index("row")
    h = lax.axis_index("col")
    chip = h // 2
    core = h % 2
    share, depth = embed.shape
    half = share // 2
    quarter = share // 4
    rows = range(groups)

    def ident(row, at, core):
        return row * col_groups + at * 2 + core

    def permute(value, pairs):
        return lax.ppermute(value, both, pairs)

    def swapped(value, axis, m):
        return lax.ppermute(value, axis, [(r, r ^ m) for r in range(lax.axis_size(axis))])

    def row_swapped(value, m):
        return swapped(value, "row", m)

    def across(value):
        return swapped(value, "col", 1)

    marg_f = marginal.astype(jnp.float32)
    logs = jnp.log(marg_f)

    plane_total = jnp.broadcast_to(jnp.sum(marg_f), (8, 128))
    step = 1
    while step < groups:
        plane_total = plane_total + row_swapped(plane_total, step)
        step *= 2

    tall = quarter + PAD
    came = []
    for c in (0, 1):
        parts = []
        for at in (c * quarter, half + c * quarter):
            under = jnp.pad(logs[at : at + quarter].reshape(1, quarter), ((0, PAD - 1), (0, depth - quarter)))
            parts += [embed[at : at + quarter], under]
        pairs = [(ident(r, q // 2, q % 2), ident(q, r, c)) for q in rows for r in rows]
        came.append(permute(jnp.concatenate(parts, axis=0), pairs))
    came = jnp.where(core == 0, came[0], came[1])
    part_row = lax.broadcasted_iota(jnp.int32, (tall, depth), 0)
    first_part = jnp.where(part_row == quarter + 1, plane_total[0, 0], came[:tall])
    second_part = came[tall:]

    def along_line(part):
        return [part] + [swapped(part, "col", 2 * d) for d in range(1, groups)]

    mine = jnp.concatenate(along_line(first_part), axis=0)
    theirs = across(mine)

    under = jnp.pad(logs.reshape(share // depth, depth), ((0, PAD - share // depth), (0, 0)))
    under = jnp.where(lax.broadcasted_iota(jnp.int32, under.shape, 0) == PAD - 1, plane_total[:, :1], under)
    coded = jnp.concatenate([embed, under], axis=0)
    pieces = {0: [coded]}
    layout = [(0, 0, share + PAD)]
    for m in range(1, groups):
        if m & (m - 1) == 0 or groups != 4:
            pieces[m] = [row_swapped(coded, m)]
            layout.append((m, 0, share + PAD))
    if groups == 4:
        pieces[3] = [row_swapped(pieces[2][0][:half], 1), row_swapped(pieces[1][0][half:], 2)]
        layout += [(3, 0, half), (3, half, half + PAD)]
    held = [pieces[m][start > 0] for m, start, _ in layout]

    listing = tile_list.reshape(-1)
    listed = jnp.sum((listing[None, :] == jnp.arange(listing.shape[0])[:, None]).astype(jnp.int32), axis=1)
    place = jnp.stack([g, chip, core]).astype(jnp.int32)

    def from_line(outs):
        summed = outs[0] + across(outs[1])
        parts = [summed[d * quarter : (d + 1) * quarter] for d in rows]
        total = parts[0]
        for d in range(1, groups):
            total = total + swapped(parts[d], "col", 2 * d)
        return summed, total

    def to_home(total):
        homes = []
        for c in (0, 1):
            homes.append(permute(total, [(ident(q, r, c), ident(r, q // 2, q % 2)) for q in rows for r in rows]))
        return homes

    tiles = [(row, col) for row in range(groups * share // BLOCK) for col in range(groups * share // BLOCK)]
    grads = functools.partial(half_grads, groups=groups, share=share, layout=layout, place=place, listed=listed, cooc=cooc)
    outs = grads(0, tiles=tiles, mine=mine, theirs=theirs, held=held, row_in=None, ready=[])
    first_summed, first_total = from_line(outs)
    parts = along_line(second_part)
    parts[1] = jnp.where(part_row == quarter + 2, outs[0][:tall], parts[1])
    mine = jnp.concatenate(parts, axis=0)
    theirs = across(mine)
    grads = functools.partial(grads, 1, mine=mine, theirs=theirs)
    columns = outs[2:5]
    outs = grads(tiles=tiles[:-1], held=outs[2:], row_in=None, ready=[first_summed])
    outs = grads(tiles=tiles[-1:], held=[*columns, outs[1]], row_in=outs[0], ready=[first_total])
    second_summed, second_total = from_line(outs)
    first_quarters = to_home(first_total)
    quarters = first_quarters + to_home(second_total)

    halves = outs[2:]
    if groups == 4:
        spare = second_summed[:PAD] + first_quarters[0][:PAD] + first_quarters[1][:PAD]
        first_x = row_swapped(jnp.concatenate([halves[2], halves[6], spare], axis=0), 1)[: 2 * half]
        first_y = row_swapped(jnp.concatenate([halves[5], halves[7], spare], axis=0), 2)[: 2 * half]
        second_x = row_swapped(halves[3] + first_y[half:], 1)
        second_y = row_swapped(halves[4] + first_x[half:], 2)
        top = halves[0] + first_x[:half] + second_y
        bottom = halves[1] + second_x + first_y[:half]
    else:
        top, bottom = halves[:2]
        for m in range(1, groups):
            top = top + row_swapped(halves[2 * m], m)
            bottom = bottom + row_swapped(halves[2 * m + 1], m)
    gradients = (jnp.concatenate([top, bottom], axis=0) + jnp.concatenate(quarters, axis=0)) / BLOCK
    new_accum = accum + gradients * gradients
    new_embed = embed - LEARN_RATE * gradients / jnp.sqrt(new_accum)
    return (new_embed, new_accum)


def solution(mesh):
    placed = (
        P("row", "col"),
        P("row", "col", None),
        P(("col", "row")),
        P(("col", "row"), None),
        P(("col", "row"), None),
    )
    return jax.shard_map(
        functools.partial(local, mesh.shape["row"], mesh.shape["col"]),
        mesh=mesh,
        in_specs=placed,
        out_specs=(P(("col", "row"), None), P(("col", "row"), None)),
        check_vma=False,
    )
```

```python
import functools

import jax
import jax.numpy as jnp
from jax import lax
from jax.experimental import pallas as pl
from jax.experimental.pallas import tpu as pltpu
from jax.sharding import PartitionSpec as P

BLOCK = 1024
LEARN_RATE = 0.05
SUB = 512
PAD = 8
VMEM_LIMIT = 42 * 2**20


def split_bf16(values):
    high = values.astype(jnp.bfloat16)
    low = (values - high.astype(jnp.float32)).astype(jnp.bfloat16)
    return high, low


def product(left, right, dims):
    (left_at,), (right_at,) = dims
    left = jnp.concatenate([left[0], left[1], left[0]], axis=left_at)
    right = jnp.concatenate([right[0], right[0], right[1]], axis=right_at)
    return lax.dot_general(left, right, (dims, ((), ())), preferred_element_type=jnp.float32)


def order_of(count):
    order = [0]
    step = count // 2
    while step:
        order += [d + step for d in order]
        step //= 2
    return order


def half_kernel(k, groups, share, layout, tiles, first, added, ends, last, extra, *refs):
    rest = list(refs)
    take = lambda count: [rest.pop(0) for _ in range(count)]
    place_ref, listed_ref, cooc_ref = take(3)
    row_refs = take(4)
    order = order_of(groups)
    if first:
        pieces = take(len(layout))
    else:
        high_ref, low_ref, log_ref, sums_in = take(4)
    if added:
        (row_in,) = take(1)
    take(extra)
    if ends:
        mine_out, other_out = take(2)
    else:
        (row_out,) = take(1)
    if first:
        high_ref, low_ref, log_ref = take(3)
    if last:
        outs = take(2 * groups)
    else:
        (sums,) = take(1)
    row_vecs, row_logs, cells, cell_sems = take(4)
    if ends:
        (row_out,) = take(1)
    if last:
        (sums,) = take(1)

    depth = row_vecs.shape[1]
    half = share // 2
    quarter = share // 4
    cols = groups * share
    col_blocks = cols // BLOCK
    per = BLOCK // share
    tall = BLOCK // 2
    g = place_ref[0]
    chip = place_ref[1]
    core = place_ref[2]

    def cell_copies(row, col):
        number = tiles.index((row, col))
        return [
            pltpu.make_async_copy(
                cooc_ref.at[pl.ds((row * per + j) * share + k * half, half), pl.ds(col * BLOCK, BLOCK)],
                cells.at[number, pl.ds(j * half, half), :],
                cell_sems.at[number, j],
            )
            for j in range(per)
        ]

    for row, col in tiles:

        @pl.when(listed_ref[row * col_blocks + col] > 0)
        def _():
            for copy in cell_copies(row, col):
                copy.start()

    if first:
        total = jnp.zeros((1, 128), jnp.float32)
        for ref in row_refs:
            for j in range(groups // 2):
                at = j * (quarter + PAD) + quarter + 1
                total = total + ref[at : at + 1, :128]
        log_total = jnp.concatenate([jnp.log(total)] * (depth // 128), axis=1)
        for piece, (other, start, count) in zip(pieces, layout):
            body = min(count, share - start)
            at = pl.multiple_of((g ^ other) * share + start, 16)
            high, low = split_bf16(piece[:body, :])
            high_ref[pl.ds(at, body), :] = high
            low_ref[pl.ds(at, body), :] = low
            if body < count:
                at = pl.multiple_of((g ^ other) * PAD, PAD)
                log_ref[pl.ds(at, PAD), :] = piece[body:, :] - log_total
        sums[...] = jnp.zeros_like(sums)
    else:
        sums[...] = sums_in[...]

    for number, ref in enumerate(row_refs):
        side = core if number < 2 else 1 - core
        for j in range(groups // 2):
            d = order[number % 2 * (groups // 2) + j]
            start = j * (quarter + PAD)
            at = pl.multiple_of((chip ^ d) * half + side * quarter, quarter)
            row_vecs[pl.ds(at, quarter), :] = ref[start : start + quarter, :]
            log_row = ref[start + quarter : start + quarter + 1, :128]
            row_logs[pl.ds(at, quarter), :] = jnp.transpose(jnp.broadcast_to(log_row, (128, 128)))[:quarter, :]
    row_out[...] = row_in[...] if added else jnp.zeros_like(row_out)

    for row, col in tiles:
        tall_rows = slice(row * tall, (row + 1) * tall)

        @pl.when(listed_ref[row * col_blocks + col] > 0)
        def _():
            for copy in cell_copies(row, col):
                copy.wait()
            rows = row_vecs[tall_rows, :]
            row_pair = split_bf16(rows)
            row_turned = split_bf16(jnp.transpose(rows))
            row_log = jnp.concatenate([row_logs[tall_rows, :]] * (SUB // 128), axis=1)
            strips = BLOCK // SUB

            def col_pair(strip):
                at = col * BLOCK + strip * SUB
                return high_ref[at : at + SUB, :], low_ref[at : at + SUB, :]

            def scores(strip):
                return product(row_pair, col_pair(strip), ((1,), (1,)))

            def slopes(strip, values):
                at = col * BLOCK + strip * SUB
                log_rows = [lane // share * PAD + lane % share // depth for lane in range(at, at + SUB, depth)]
                col_log = jnp.concatenate([log_ref[q : q + 1, :] for q in log_rows], axis=1)
                centred = values + row_log + col_log
                counts = cells[tiles.index((row, col)), :, strip * SUB : (strip + 1) * SUB]
                counts_f = counts.astype(jnp.float32)
                floor = jnp.maximum(counts_f, 1.0)
                weights = 0.1 + 0.25 * (counts_f * lax.rsqrt(floor))
                return split_bf16(
                    jnp.where(
                        counts_f > 0,
                        weights * (centred - jnp.log(floor)),
                        0.5 * jnp.tanh(0.5 * centred) + 0.5,
                    )
                )

            def gradients(strip, pair):
                at = col * BLOCK + strip * SUB
                row_out[tall_rows, :] += product(pair, col_pair(strip), ((1,), (0,)))
                sums[:, at : at + SUB] += product(row_turned, pair, ((1,), (0,)))

            ahead = scores(0)
            behind = None
            for strip in range(strips):
                values = ahead
                if strip + 1 < strips:
                    ahead = scores(strip + 1)
                if strip > 0:
                    gradients(strip - 1, behind)
                behind = slopes(strip, values)
            gradients(strips - 1, behind)

    for out, side in ((mine_out, core), (other_out, 1 - core)) if ends else ():
        for j, d in enumerate(order):
            at = pl.multiple_of((chip ^ d) * half + side * quarter, quarter)
            out[j * quarter : (j + 1) * quarter, :] = row_out[pl.ds(at, quarter), :]
    if last:
        for other in range(groups):
            at = pl.multiple_of((g ^ other) * share, share)
            block = jnp.transpose(sums[:, pl.ds(at, share)])
            outs[2 * other][...] = block[:half]
            outs[2 * other + 1][...] = block[half:]


def half_grads(k, groups, share, layout, tiles, place, listed, cooc, vectors, held, row_in, ready):
    depth = vectors[0].shape[1]
    cols = groups * share
    first = k == 0 and tiles[0] == (0, 0)
    added = row_in is not None
    ends = tiles[-1] == (cols // BLOCK - 1,) * 2
    last = ends and k == 1
    per = BLOCK // share
    rows = groups * share // 2
    whole = pl.BlockSpec(memory_space=pltpu.VMEM)
    scalar = pl.BlockSpec(memory_space=pltpu.SMEM)
    remote = pl.BlockSpec(memory_space=pl.ANY)
    row_part = jax.ShapeDtypeStruct((rows // 2, depth), jnp.float32)
    row_all = jax.ShapeDtypeStruct((rows, depth), jnp.float32)
    col_half = jax.ShapeDtypeStruct((share // 2, depth), jnp.float32)
    coded = jax.ShapeDtypeStruct((cols, depth), jnp.bfloat16)
    logs = jax.ShapeDtypeStruct((groups * PAD, depth), jnp.float32)
    turned = jax.ShapeDtypeStruct((depth, cols), jnp.float32)
    out_shape = [row_part] * 2 if ends else [row_all]
    out_shape += [coded, coded, logs] if first else []
    out_shape += [col_half] * (2 * groups) if last else [turned]
    held = [*held, row_in] if added else [*held]
    args = [place, listed, cooc, *vectors, *held, *ready]
    in_specs = [scalar] * 2 + [remote] + [whole] * (4 + len(held)) + [remote] * len(ready)
    scratch = [
        pltpu.VMEM((rows, depth), jnp.float32),
        pltpu.VMEM((rows, 128), jnp.float32),
        pltpu.VMEM((len(tiles), BLOCK // 2, BLOCK), jnp.int32),
        pltpu.SemaphoreType.DMA((len(tiles), per)),
    ]
    if ends:
        scratch.append(pltpu.VMEM((rows, depth), jnp.float32))
    if last:
        scratch.append(pltpu.VMEM((depth, cols), jnp.float32))
    cells = len(tiles) * BLOCK * BLOCK // 2
    return pl.pallas_call(
        functools.partial(half_kernel, k, groups, share, layout, tiles, first, added, ends, last, len(ready)),
        out_shape=out_shape,
        in_specs=in_specs,
        out_specs=[whole] * len(out_shape),
        scratch_shapes=scratch,
        compiler_params=pltpu.CompilerParams(vmem_limit_bytes=VMEM_LIMIT),
        cost_estimate=pl.CostEstimate(
            flops=cells * depth * 18, bytes_accessed=4 * cells + 8 * cols * depth, transcendentals=3 * cells
        ),
        name="half_grads",
    )(*args)


def local(groups, col_groups, cooc, tile_list, marginal, embed, accum):
    assert col_groups == 2 * groups and groups & (groups - 1) == 0
    both = ("row", "col")
    g = lax.axis_index("row")
    h = lax.axis_index("col")
    chip = h // 2
    core = h % 2
    share, depth = embed.shape
    half = share // 2
    quarter = share // 4
    rows = range(groups)

    def ident(row, at, core):
        return row * col_groups + at * 2 + core

    def permute(value, pairs):
        return lax.ppermute(value, both, pairs)

    def swapped(value, axis, m):
        return lax.ppermute(value, axis, [(r, r ^ m) for r in range(lax.axis_size(axis))])

    def row_swapped(value, m):
        return swapped(value, "row", m)

    def across(value):
        return swapped(value, "col", 1)

    marg_f = marginal.astype(jnp.float32)
    logs = jnp.log(marg_f)

    plane_total = jnp.broadcast_to(jnp.sum(marg_f), (8, 128))
    step = 1
    while step < groups:
        plane_total = plane_total + row_swapped(plane_total, step)
        step *= 2

    def to_line(k):
        came = []
        for c in (0, 1):
            at = k * half + c * quarter
            under = jnp.pad(logs[at : at + quarter].reshape(1, quarter), ((0, PAD - 1), (0, depth - quarter)))
            part = jnp.concatenate([embed[at : at + quarter], under], axis=0)
            came.append(permute(part, [(ident(r, q // 2, q % 2), ident(q, r, c)) for q in rows for r in rows]))
        return jnp.where(core == 0, came[0], came[1])

    def along_line(part, after=()):
        step = groups // 2
        while step > 1:
            came = swapped(part, "col", 2 * step)
            part = part[: part.shape[0] - 2 * len(after)]
            part = jnp.concatenate([part, *[array[:2] for array in after], came], axis=0)
            after = ()
            step //= 2
        return part, swapped(part, "col", 2)

    under = jnp.pad(logs.reshape(share // depth, depth), ((0, PAD - share // depth), (0, 0)))
    coded = jnp.concatenate([embed, under], axis=0)
    pieces = {0: [coded]}
    layout = [(0, 0, share + PAD)]
    for m in range(1, groups):
        if m & (m - 1) == 0 or groups != 4:
            pieces[m] = [row_swapped(coded, m)]
            layout.append((m, 0, share + PAD))
    if groups == 4:
        pieces[3] = [row_swapped(pieces[2][0][:half], 1), row_swapped(pieces[1][0][half:], 2)]
        layout += [(3, 0, half), (3, half, half + PAD)]
    held = [pieces[m][start > 0] for m, start, _ in layout]

    part = to_line(0)
    part_row = lax.broadcasted_iota(jnp.int32, part.shape, 0)
    part = jnp.where(part_row == quarter + 1, plane_total[0, 0], part)
    for number, m in enumerate([1 << q for q in range(groups.bit_length() - 1)]):
        part = jnp.where(part_row == quarter + 2 + number, pieces[m][0][: quarter + PAD], part)
    lower, upper = along_line(part, pieces[3] if groups == 4 else ())
    vectors = [lower, upper, across(lower), across(upper)]

    listing = tile_list.reshape(-1)
    listed = jnp.sum((listing[None, :] == jnp.arange(listing.shape[0])[:, None]).astype(jnp.int32), axis=1)
    place = jnp.stack([g, chip, core]).astype(jnp.int32)

    def from_line(outs):
        summed = total = outs[0] + across(outs[1])
        step = 1
        while step < groups:
            kept = total.shape[0] // 2
            total = total[:kept] + swapped(total[kept:], "col", 2 * step)
            step *= 2
        return summed, total

    def to_home(total):
        homes = []
        for c in (0, 1):
            homes.append(permute(total, [(ident(q, r, c), ident(r, q // 2, q % 2)) for q in rows for r in rows]))
        return homes

    tiles = [(row, col) for row in range(groups * share // BLOCK) for col in range(groups * share // BLOCK)]
    grads = functools.partial(half_grads, groups=groups, share=share, layout=layout, place=place, listed=listed, cooc=cooc)
    lower, upper = along_line(to_line(1))
    outs = grads(0, tiles=tiles[:-1], vectors=vectors, held=held, row_in=None, ready=[lower])
    columns = outs[1:4]
    outs = grads(0, tiles=tiles[-1:], vectors=vectors, held=outs[1:], row_in=outs[0], ready=[upper])
    first_summed, first_total = from_line(outs)
    vectors = [lower, upper, across(lower), across(upper)]
    outs = grads(1, tiles=tiles[:-1], vectors=vectors, held=[*columns, outs[2]], row_in=None, ready=[first_summed])
    outs = grads(1, tiles=tiles[-1:], vectors=vectors, held=[*columns, outs[1]], row_in=outs[0], ready=[first_total])
    second_summed, second_total = from_line(outs)
    first_quarters = to_home(first_total)
    quarters = first_quarters + to_home(second_total)

    halves = outs[2:]
    if groups == 4:
        spare = second_summed[:PAD]
        first_x = row_swapped(jnp.concatenate([halves[2], halves[6], spare], axis=0), 1)[: 2 * half]
        first_y = row_swapped(jnp.concatenate([halves[5], halves[7], spare], axis=0), 2)[: 2 * half]
        second_x = row_swapped(halves[3] + first_y[half:], 1)
        second_y = row_swapped(halves[4] + first_x[half:], 2)
        top = halves[0] + first_x[:half] + second_y
        bottom = halves[1] + second_x + first_y[:half]
    else:
        top, bottom = halves[:2]
        for m in range(1, groups):
            top = top + row_swapped(halves[2 * m], m)
            bottom = bottom + row_swapped(halves[2 * m + 1], m)
    gradients = (jnp.concatenate([top, bottom], axis=0) + jnp.concatenate(quarters, axis=0)) / BLOCK
    new_accum = accum + gradients * gradients
    new_embed = embed - LEARN_RATE * gradients / jnp.sqrt(new_accum)
    return (new_embed, new_accum)


def solution(mesh):
    placed = (
        P("row", "col"),
        P("row", "col", None),
        P(("col", "row")),
        P(("col", "row"), None),
        P(("col", "row"), None),
    )
    return jax.shard_map(
        functools.partial(local, mesh.shape["row"], mesh.shape["col"]),
        mesh=mesh,
        in_specs=placed,
        out_specs=(P(("col", "row"), None), P(("col", "row"), None)),
        check_vma=False,
    )
```

```python
import functools

import jax
import jax.numpy as jnp
from jax import lax
from jax.experimental import pallas as pl
from jax.experimental.pallas import tpu as pltpu
from jax.sharding import PartitionSpec as P

BLOCK = 1024
LEARN_RATE = 0.05
SUB = 512
PAD = 8
VMEM_LIMIT = 42 * 2**20


def split_bf16(values):
    high = values.astype(jnp.bfloat16)
    low = (values - high.astype(jnp.float32)).astype(jnp.bfloat16)
    return high, low


def product(left, right, dims):
    (left_at,), (right_at,) = dims
    left = jnp.concatenate([left[0], left[1], left[0]], axis=left_at)
    right = jnp.concatenate([right[0], right[0], right[1]], axis=right_at)
    return lax.dot_general(left, right, (dims, ((), ())), preferred_element_type=jnp.float32)


def order_of(count):
    order = [0]
    step = count // 2
    while step:
        order += [d + step for d in order]
        step //= 2
    return order


def half_kernel(k, groups, share, layout, tiles, first, added, ends, last, extra, *refs):
    rest = list(refs)
    take = lambda count: [rest.pop(0) for _ in range(count)]
    place_ref, listed_ref, cooc_ref = take(3)
    row_refs = take(4)
    order = order_of(groups)
    if first:
        pieces = take(len(layout))
    else:
        high_ref, low_ref, log_ref, sums_in = take(4)
    if added:
        (row_in,) = take(1)
    take(extra)
    if ends:
        mine_out, other_out = take(2)
    else:
        (row_out,) = take(1)
    if first:
        high_ref, low_ref, log_ref = take(3)
    if last:
        outs = take(2 * groups)
    else:
        (sums,) = take(1)
    row_vecs, row_logs, cells, cell_sems = take(4)
    if ends:
        (row_out,) = take(1)
    if last:
        (sums,) = take(1)

    depth = row_vecs.shape[1]
    half = share // 2
    quarter = share // 4
    cols = groups * share
    col_blocks = cols // BLOCK
    per = BLOCK // share
    tall = BLOCK // 2
    g = place_ref[0]
    chip = place_ref[1]
    core = place_ref[2]

    def cell_copies(row, col):
        number = tiles.index((row, col))
        return [
            pltpu.make_async_copy(
                cooc_ref.at[pl.ds((row * per + j) * share + k * half, half), pl.ds(col * BLOCK, BLOCK)],
                cells.at[number, pl.ds(j * half, half), :],
                cell_sems.at[number, j],
            )
            for j in range(per)
        ]

    for row, col in tiles:

        @pl.when(listed_ref[row * col_blocks + col] > 0)
        def _():
            for copy in cell_copies(row, col):
                copy.start()

    if first:
        total = jnp.zeros((1, 128), jnp.float32)
        for ref in row_refs:
            for j in range(groups // 2):
                at = j * (quarter + PAD) + quarter + 1
                total = total + ref[at : at + 1, :128]
        log_total = jnp.concatenate([jnp.log(total)] * (depth // 128), axis=1)
        for piece, (other, start, count) in zip(pieces, layout):
            body = min(count, share - start)
            at = pl.multiple_of((g ^ other) * share + start, 16)
            high, low = split_bf16(piece[:body, :])
            high_ref[pl.ds(at, body), :] = high
            low_ref[pl.ds(at, body), :] = low
            if body < count:
                at = pl.multiple_of((g ^ other) * PAD, PAD)
                log_ref[pl.ds(at, PAD), :] = piece[body:, :] - log_total
        sums[...] = jnp.zeros_like(sums)
    else:
        sums[...] = sums_in[...]

    for number, ref in enumerate(row_refs):
        side = core if number < 2 else 1 - core
        for j in range(groups // 2):
            d = order[number % 2 * (groups // 2) + j]
            start = j * (quarter + PAD)
            at = pl.multiple_of((chip ^ d) * half + side * quarter, quarter)
            row_vecs[pl.ds(at, quarter), :] = ref[start : start + quarter, :]
            log_row = ref[start + quarter : start + quarter + 1, :128]
            row_logs[pl.ds(at, quarter), :] = jnp.transpose(jnp.broadcast_to(log_row, (128, 128)))[:quarter, :]
    row_out[...] = row_in[...] if added else jnp.zeros_like(row_out)

    for row, col in tiles:
        tall_rows = slice(row * tall, (row + 1) * tall)

        @pl.when(listed_ref[row * col_blocks + col] > 0)
        def _():
            for copy in cell_copies(row, col):
                copy.wait()
            rows = row_vecs[tall_rows, :]
            row_pair = split_bf16(rows)
            row_turned = split_bf16(jnp.transpose(rows))
            row_log = jnp.concatenate([row_logs[tall_rows, :]] * (SUB // 128), axis=1)
            strips = BLOCK // SUB

            def col_pair(strip):
                at = col * BLOCK + strip * SUB
                return high_ref[at : at + SUB, :], low_ref[at : at + SUB, :]

            def scores(strip):
                return product(row_pair, col_pair(strip), ((1,), (1,)))

            def slopes(strip, values):
                at = col * BLOCK + strip * SUB
                log_rows = [lane // share * PAD + lane % share // depth for lane in range(at, at + SUB, depth)]
                col_log = jnp.concatenate([log_ref[q : q + 1, :] for q in log_rows], axis=1)
                centred = values + row_log + col_log
                counts = cells[tiles.index((row, col)), :, strip * SUB : (strip + 1) * SUB]
                counts_f = counts.astype(jnp.float32)
                floor = jnp.maximum(counts_f, 1.0)
                weights = 0.1 + 0.25 * (counts_f * lax.rsqrt(floor))
                return split_bf16(
                    jnp.where(
                        counts_f > 0,
                        weights * (centred - jnp.log(floor)),
                        0.5 * jnp.tanh(0.5 * centred) + 0.5,
                    )
                )

            def gradients(strip, pair):
                at = col * BLOCK + strip * SUB
                row_out[tall_rows, :] += product(pair, col_pair(strip), ((1,), (0,)))
                sums[:, at : at + SUB] += product(row_turned, pair, ((1,), (0,)))

            ahead = scores(0)
            behind = None
            for strip in range(strips):
                values = ahead
                if strip + 1 < strips:
                    ahead = scores(strip + 1)
                if strip > 0:
                    gradients(strip - 1, behind)
                behind = slopes(strip, values)
            gradients(strips - 1, behind)

    for out, side in ((mine_out, core), (other_out, 1 - core)) if ends else ():
        for j, d in enumerate(order):
            at = pl.multiple_of((chip ^ d) * half + side * quarter, quarter)
            out[j * quarter : (j + 1) * quarter, :] = row_out[pl.ds(at, quarter), :]
    if last:
        for other in range(groups):
            at = pl.multiple_of((g ^ other) * share, share)
            block = jnp.transpose(sums[:, pl.ds(at, share)])
            outs[2 * other][...] = block[:half]
            outs[2 * other + 1][...] = block[half:]


def half_grads(k, groups, share, layout, tiles, place, listed, cooc, vectors, held, row_in, ready):
    depth = vectors[0].shape[1]
    cols = groups * share
    first = k == 0 and tiles[0] == (0, 0)
    added = row_in is not None
    ends = tiles[-1] == (cols // BLOCK - 1,) * 2
    last = ends and k == 1
    per = BLOCK // share
    rows = groups * share // 2
    whole = pl.BlockSpec(memory_space=pltpu.VMEM)
    scalar = pl.BlockSpec(memory_space=pltpu.SMEM)
    remote = pl.BlockSpec(memory_space=pl.ANY)
    row_part = jax.ShapeDtypeStruct((rows // 2, depth), jnp.float32)
    row_all = jax.ShapeDtypeStruct((rows, depth), jnp.float32)
    col_half = jax.ShapeDtypeStruct((share // 2, depth), jnp.float32)
    coded = jax.ShapeDtypeStruct((cols, depth), jnp.bfloat16)
    logs = jax.ShapeDtypeStruct((groups * PAD, depth), jnp.float32)
    turned = jax.ShapeDtypeStruct((depth, cols), jnp.float32)
    out_shape = [row_part] * 2 if ends else [row_all]
    out_shape += [coded, coded, logs] if first else []
    out_shape += [col_half] * (2 * groups) if last else [turned]
    held = [*held, row_in] if added else [*held]
    args = [place, listed, cooc, *vectors, *held, *ready]
    in_specs = [scalar] * 2 + [remote] + [whole] * (4 + len(held)) + [remote] * len(ready)
    scratch = [
        pltpu.VMEM((rows, depth), jnp.float32),
        pltpu.VMEM((rows, 128), jnp.float32),
        pltpu.VMEM((len(tiles), BLOCK // 2, BLOCK), jnp.int32),
        pltpu.SemaphoreType.DMA((len(tiles), per)),
    ]
    if ends:
        scratch.append(pltpu.VMEM((rows, depth), jnp.float32))
    if last:
        scratch.append(pltpu.VMEM((depth, cols), jnp.float32))
    cells = len(tiles) * BLOCK * BLOCK // 2
    return pl.pallas_call(
        functools.partial(half_kernel, k, groups, share, layout, tiles, first, added, ends, last, len(ready)),
        out_shape=out_shape,
        in_specs=in_specs,
        out_specs=[whole] * len(out_shape),
        scratch_shapes=scratch,
        compiler_params=pltpu.CompilerParams(vmem_limit_bytes=VMEM_LIMIT),
        cost_estimate=pl.CostEstimate(
            flops=cells * depth * 18, bytes_accessed=4 * cells + 8 * cols * depth, transcendentals=3 * cells
        ),
        name="half_grads",
    )(*args)


def local(groups, col_groups, cooc, tile_list, marginal, embed, accum):
    assert col_groups == 2 * groups and groups & (groups - 1) == 0
    both = ("row", "col")
    g = lax.axis_index("row")
    h = lax.axis_index("col")
    chip = h // 2
    core = h % 2
    share, depth = embed.shape
    half = share // 2
    quarter = share // 4
    rows = range(groups)

    def ident(row, at, core):
        return row * col_groups + at * 2 + core

    def permute(value, pairs):
        return lax.ppermute(value, both, pairs)

    def swapped(value, axis, m):
        return lax.ppermute(value, axis, [(r, r ^ m) for r in range(lax.axis_size(axis))])

    def row_swapped(value, m):
        return swapped(value, "row", m)

    def across(value):
        return swapped(value, "col", 1)

    marg_f = marginal.astype(jnp.float32)
    logs = jnp.log(marg_f)

    plane_total = jnp.broadcast_to(jnp.sum(marg_f), (8, 128))
    step = 1
    while step < groups:
        plane_total = plane_total + row_swapped(plane_total, step)
        step *= 2

    last_spare = lax.broadcasted_iota(jnp.int32, (PAD, depth), 0) == PAD - 1

    def to_line(k, after):
        came = []
        for c in (0, 1):
            at = k * half + c * quarter
            under = jnp.pad(logs[at : at + quarter].reshape(1, quarter), ((0, PAD - 1), (0, depth - quarter)))
            under = jnp.where(last_spare, after, under)
            part = jnp.concatenate([embed[at : at + quarter], under], axis=0)
            came.append(permute(part, [(ident(r, q // 2, q % 2), ident(q, r, c)) for q in rows for r in rows]))
        return jnp.where(core == 0, came[0], came[1])

    def along_line_at_once(part):
        came = [swapped(part, "col", 2 * d) for d in range(1, groups)]
        parts = [([part] + came)[d] for d in order_of(groups)]
        return [jnp.concatenate(few, axis=0) for few in (parts[: groups // 2], parts[groups // 2 :])] + [came]

    def along_line(part, after):
        step = groups // 2
        first_came = None
        while step > 1:
            came = swapped(part, "col", 2 * step)
            first_came = came if first_came is None else first_came
            part = part[: part.shape[0] - 2 * len(after)]
            part = jnp.concatenate([part, *[array[:2] for array in after], came], axis=0)
            after = ()
            step //= 2
        return part, swapped(part, "col", 2), first_came

    under = jnp.pad(logs.reshape(share // depth, depth), ((0, PAD - share // depth), (0, 0)))
    under = jnp.where(lax.broadcasted_iota(jnp.int32, (PAD, depth), 0) == PAD - 1, plane_total[:, :1], under)
    coded = jnp.concatenate([embed, under], axis=0)
    pieces = {0: [coded]}
    layout = [(0, 0, share + PAD)]
    for m in range(1, groups):
        if m & (m - 1) == 0 or groups != 4:
            pieces[m] = [row_swapped(coded, m)]
            layout.append((m, 0, share + PAD))
    if groups == 4:
        pieces[3] = [row_swapped(pieces[2][0][:half], 1), row_swapped(pieces[1][0][half:], 2)]
        layout += [(3, 0, half), (3, half, half + PAD)]
    held = [pieces[m][start > 0] for m, start, _ in layout]

    part = to_line(0, plane_total[:, :1])
    part_row = lax.broadcasted_iota(jnp.int32, part.shape, 0)
    part = jnp.where(part_row == quarter + 1, plane_total[0, 0], part)
    for number, m in enumerate([1 << q for q in range(groups.bit_length() - 1)]):
        part = jnp.where(part_row == quarter + 2 + number, pieces[m][0][: quarter + PAD], part)
    lower, upper, first_came = along_line(part, pieces[3] if groups == 4 else ())
    vectors = [lower, upper, across(lower), across(upper)]

    listing = tile_list.reshape(-1)
    listed = jnp.sum((listing[None, :] == jnp.arange(listing.shape[0])[:, None]).astype(jnp.int32), axis=1)
    place = jnp.stack([g, chip, core]).astype(jnp.int32)

    def from_line_at_once(outs):
        summed = outs[0] + across(outs[1])
        parts = {d: summed[j * quarter : (j + 1) * quarter] for j, d in enumerate(order_of(groups))}
        total = parts[0]
        for d in range(1, groups):
            total = total + swapped(parts[d], "col", 2 * d)
        return summed, total

    def from_line(outs):
        summed = total = outs[0] + across(outs[1])
        step = 1
        while step < groups:
            kept = total.shape[0] // 2
            came = swapped(total[kept:], "col", 2 * step)
            first_came = came if step == 1 else first_came
            total = total[:kept] + came
            step *= 2
        return summed, total, first_came

    def to_home(total, after=None):
        homes = []
        for c in (0, 1):
            value = total if after is None else jnp.where(core == c, total, after)
            homes.append(permute(value, [(ident(q, r, c), ident(r, q // 2, q % 2)) for q in rows for r in rows]))
        return homes

    tiles = [(row, col) for row in range(groups * share // BLOCK) for col in range(groups * share // BLOCK)]
    grads = functools.partial(half_grads, groups=groups, share=share, layout=layout, place=place, listed=listed, cooc=cooc)
    lower, upper, came = along_line_at_once(to_line(1, first_came[:PAD]))
    outs = grads(0, tiles=tiles[:-1], vectors=vectors, held=held, row_in=None, ready=[])
    columns = outs[1:4]
    outs = grads(0, tiles=tiles[-1:], vectors=vectors, held=outs[1:], row_in=outs[0], ready=came)
    first_summed, first_total = from_line_at_once(outs)
    vectors = [lower, upper, across(lower), across(upper)]
    outs = grads(1, tiles=tiles[:-1], vectors=vectors, held=[*columns, outs[2]], row_in=None, ready=[first_summed])
    outs = grads(1, tiles=tiles[-1:], vectors=vectors, held=[*columns, outs[1]], row_in=outs[0], ready=[first_total])
    second_summed, second_total, second_came = from_line(outs)
    first_quarters = to_home(first_total, second_came[:quarter])
    quarters = first_quarters + to_home(second_total)

    halves = outs[2:]
    if groups == 4:
        spare = second_summed[:PAD]
        first_x = row_swapped(jnp.concatenate([halves[2], halves[6], spare], axis=0), 1)[: 2 * half]
        first_y = row_swapped(jnp.concatenate([halves[5], halves[7], spare], axis=0), 2)[: 2 * half]
        second_x = row_swapped(halves[3] + first_y[half:], 1)
        second_y = row_swapped(halves[4] + first_x[half:], 2)
        top = halves[0] + first_x[:half] + second_y
        bottom = halves[1] + second_x + first_y[:half]
    else:
        top, bottom = halves[:2]
        for m in range(1, groups):
            top = top + row_swapped(halves[2 * m], m)
            bottom = bottom + row_swapped(halves[2 * m + 1], m)
    gradients = (jnp.concatenate([top, bottom], axis=0) + jnp.concatenate(quarters, axis=0)) / BLOCK
    new_accum = accum + gradients * gradients
    new_embed = embed - LEARN_RATE * gradients / jnp.sqrt(new_accum)
    return (new_embed, new_accum)


def solution(mesh):
    placed = (
        P("row", "col"),
        P("row", "col", None),
        P(("col", "row")),
        P(("col", "row"), None),
        P(("col", "row"), None),
    )
    return jax.shard_map(
        functools.partial(local, mesh.shape["row"], mesh.shape["col"]),
        mesh=mesh,
        in_specs=placed,
        out_specs=(P(("col", "row"), None), P(("col", "row"), None)),
        check_vma=False,
    )
```

```python
import functools

import jax
import jax.numpy as jnp
from jax import lax
from jax.experimental import pallas as pl
from jax.experimental.pallas import tpu as pltpu
from jax.sharding import PartitionSpec as P

BLOCK = 1024
LEARN_RATE = 0.05
SUB = 1024
PAD = 8
VMEM_LIMIT = 42 * 2**20


def split_bf16(values):
    high = values.astype(jnp.bfloat16)
    low = (values - high.astype(jnp.float32)).astype(jnp.bfloat16)
    return high, low


def product(left, right, dims):
    (left_at,), (right_at,) = dims
    left = jnp.concatenate([left[0], left[1], left[0]], axis=left_at)
    right = jnp.concatenate([right[0], right[0], right[1]], axis=right_at)
    return lax.dot_general(left, right, (dims, ((), ())), preferred_element_type=jnp.float32)


def order_of(count):
    order = [0]
    step = count // 2
    while step:
        order += [d + step for d in order]
        step //= 2
    return order


def half_kernel(k, groups, share, layout, tiles, first, added, ends, last, extra, *refs):
    rest = list(refs)
    take = lambda count: [rest.pop(0) for _ in range(count)]
    place_ref, listed_ref, cooc_ref = take(3)
    row_refs = take(4)
    order = order_of(groups)
    if first:
        pieces = take(len(layout))
    else:
        high_ref, low_ref, log_ref, sums_in = take(4)
    if added:
        (row_in,) = take(1)
    take(extra)
    if ends:
        mine_out, other_out = take(2)
    else:
        (row_out,) = take(1)
    if first:
        high_ref, low_ref, log_ref = take(3)
    if last:
        outs = take(2 * groups)
    else:
        (sums,) = take(1)
    row_vecs, row_logs, cells, cell_sems = take(4)
    if ends:
        (row_out,) = take(1)
    if last:
        (sums,) = take(1)

    depth = row_vecs.shape[1]
    half = share // 2
    quarter = share // 4
    cols = groups * share
    col_blocks = cols // BLOCK
    per = BLOCK // share
    tall = BLOCK // 2
    g = place_ref[0]
    chip = place_ref[1]
    core = place_ref[2]

    def cell_copies(row, col):
        number = tiles.index((row, col))
        return [
            pltpu.make_async_copy(
                cooc_ref.at[pl.ds((row * per + j) * share + k * half, half), pl.ds(col * BLOCK, BLOCK)],
                cells.at[number, pl.ds(j * half, half), :],
                cell_sems.at[number, j],
            )
            for j in range(per)
        ]

    for row, col in tiles:

        @pl.when(listed_ref[row * col_blocks + col] > 0)
        def _():
            for copy in cell_copies(row, col):
                copy.start()

    if first:
        total = jnp.zeros((1, 128), jnp.float32)
        for ref in row_refs:
            for j in range(groups // 2):
                at = j * (quarter + PAD) + quarter + 1
                total = total + ref[at : at + 1, :128]
        log_total = jnp.concatenate([jnp.log(total)] * (depth // 128), axis=1)
        for piece, (other, start, count) in zip(pieces, layout):
            body = min(count, share - start)
            at = pl.multiple_of((g ^ other) * share + start, 16)
            high, low = split_bf16(piece[:body, :])
            high_ref[pl.ds(at, body), :] = high
            low_ref[pl.ds(at, body), :] = low
            if body < count:
                at = pl.multiple_of((g ^ other) * PAD, PAD)
                log_ref[pl.ds(at, PAD), :] = piece[body:, :] - log_total
        sums[...] = jnp.zeros_like(sums)
    else:
        sums[...] = sums_in[...]

    for number, ref in enumerate(row_refs):
        side = core if number < 2 else 1 - core
        for j in range(groups // 2):
            d = order[number % 2 * (groups // 2) + j]
            start = j * (quarter + PAD)
            at = pl.multiple_of((chip ^ d) * half + side * quarter, quarter)
            row_vecs[pl.ds(at, quarter), :] = ref[start : start + quarter, :]
            log_row = ref[start + quarter : start + quarter + 1, :128]
            row_logs[pl.ds(at, quarter), :] = jnp.transpose(jnp.broadcast_to(log_row, (128, 128)))[:quarter, :]
    row_out[...] = row_in[...] if added else jnp.zeros_like(row_out)

    for row, col in tiles:
        tall_rows = slice(row * tall, (row + 1) * tall)

        @pl.when(listed_ref[row * col_blocks + col] > 0)
        def _():
            for copy in cell_copies(row, col):
                copy.wait()
            rows = row_vecs[tall_rows, :]
            row_pair = split_bf16(rows)
            row_turned = split_bf16(jnp.transpose(rows))
            row_log = jnp.concatenate([row_logs[tall_rows, :]] * (SUB // 128), axis=1)
            strips = BLOCK // SUB

            def col_pair(strip):
                at = col * BLOCK + strip * SUB
                return high_ref[at : at + SUB, :], low_ref[at : at + SUB, :]

            def scores(strip):
                return product(row_pair, col_pair(strip), ((1,), (1,)))

            def slopes(strip, values):
                at = col * BLOCK + strip * SUB
                log_rows = [lane // share * PAD + lane % share // depth for lane in range(at, at + SUB, depth)]
                col_log = jnp.concatenate([log_ref[q : q + 1, :] for q in log_rows], axis=1)
                centred = values + row_log + col_log
                counts = cells[tiles.index((row, col)), :, strip * SUB : (strip + 1) * SUB]
                counts_f = counts.astype(jnp.float32)
                floor = jnp.maximum(counts_f, 1.0)
                weights = 0.1 + 0.25 * (counts_f * lax.rsqrt(floor))
                return split_bf16(
                    jnp.where(
                        counts_f > 0,
                        weights * (centred - jnp.log(floor)),
                        0.5 * jnp.tanh(0.5 * centred) + 0.5,
                    )
                )

            def gradients(strip, pair):
                at = col * BLOCK + strip * SUB
                row_out[tall_rows, :] += product(pair, col_pair(strip), ((1,), (0,)))
                sums[:, at : at + SUB] += product(row_turned, pair, ((1,), (0,)))

            ahead = scores(0)
            behind = None
            for strip in range(strips):
                values = ahead
                if strip + 1 < strips:
                    ahead = scores(strip + 1)
                if strip > 0:
                    gradients(strip - 1, behind)
                behind = slopes(strip, values)
            gradients(strips - 1, behind)

    for out, side in ((mine_out, core), (other_out, 1 - core)) if ends else ():
        for j, d in enumerate(order):
            at = pl.multiple_of((chip ^ d) * half + side * quarter, quarter)
            out[j * quarter : (j + 1) * quarter, :] = row_out[pl.ds(at, quarter), :]
    if last:
        for other in range(groups):
            at = pl.multiple_of((g ^ other) * share, share)
            block = jnp.transpose(sums[:, pl.ds(at, share)])
            outs[2 * other][...] = block[:half]
            outs[2 * other + 1][...] = block[half:]


def half_grads(k, groups, share, layout, tiles, place, listed, cooc, vectors, held, row_in, ready):
    depth = vectors[0].shape[1]
    cols = groups * share
    first = k == 0 and tiles[0] == (0, 0)
    added = row_in is not None
    ends = tiles[-1] == (cols // BLOCK - 1,) * 2
    last = ends and k == 1
    per = BLOCK // share
    rows = groups * share // 2
    whole = pl.BlockSpec(memory_space=pltpu.VMEM)
    scalar = pl.BlockSpec(memory_space=pltpu.SMEM)
    remote = pl.BlockSpec(memory_space=pl.ANY)
    row_part = jax.ShapeDtypeStruct((rows // 2, depth), jnp.float32)
    row_all = jax.ShapeDtypeStruct((rows, depth), jnp.float32)
    col_half = jax.ShapeDtypeStruct((share // 2, depth), jnp.float32)
    coded = jax.ShapeDtypeStruct((cols, depth), jnp.bfloat16)
    logs = jax.ShapeDtypeStruct((groups * PAD, depth), jnp.float32)
    turned = jax.ShapeDtypeStruct((depth, cols), jnp.float32)
    out_shape = [row_part] * 2 if ends else [row_all]
    out_shape += [coded, coded, logs] if first else []
    out_shape += [col_half] * (2 * groups) if last else [turned]
    held = [*held, row_in] if added else [*held]
    args = [place, listed, cooc, *vectors, *held, *ready]
    in_specs = [scalar] * 2 + [remote] + [whole] * (4 + len(held)) + [remote] * len(ready)
    scratch = [
        pltpu.VMEM((rows, depth), jnp.float32),
        pltpu.VMEM((rows, 128), jnp.float32),
        pltpu.VMEM((len(tiles), BLOCK // 2, BLOCK), jnp.int32),
        pltpu.SemaphoreType.DMA((len(tiles), per)),
    ]
    if ends:
        scratch.append(pltpu.VMEM((rows, depth), jnp.float32))
    if last:
        scratch.append(pltpu.VMEM((depth, cols), jnp.float32))
    cells = len(tiles) * BLOCK * BLOCK // 2
    return pl.pallas_call(
        functools.partial(half_kernel, k, groups, share, layout, tiles, first, added, ends, last, len(ready)),
        out_shape=out_shape,
        in_specs=in_specs,
        out_specs=[whole] * len(out_shape),
        scratch_shapes=scratch,
        compiler_params=pltpu.CompilerParams(vmem_limit_bytes=VMEM_LIMIT),
        cost_estimate=pl.CostEstimate(
            flops=cells * depth * 18, bytes_accessed=4 * cells + 8 * cols * depth, transcendentals=3 * cells
        ),
        name="half_grads",
    )(*args)


def local(groups, col_groups, cooc, tile_list, marginal, embed, accum):
    assert col_groups == 2 * groups and groups & (groups - 1) == 0
    both = ("row", "col")
    g = lax.axis_index("row")
    h = lax.axis_index("col")
    chip = h // 2
    core = h % 2
    share, depth = embed.shape
    half = share // 2
    quarter = share // 4
    rows = range(groups)

    def ident(row, at, core):
        return row * col_groups + at * 2 + core

    def permute(value, pairs):
        return lax.ppermute(value, both, pairs)

    def swapped(value, axis, m):
        return lax.ppermute(value, axis, [(r, r ^ m) for r in range(lax.axis_size(axis))])

    def row_swapped(value, m):
        return swapped(value, "row", m)

    def across(value):
        return swapped(value, "col", 1)

    marg_f = marginal.astype(jnp.float32)
    logs = jnp.log(marg_f)

    plane_total = jnp.broadcast_to(jnp.sum(marg_f), (8, 128))
    step = 1
    while step < groups:
        plane_total = plane_total + row_swapped(plane_total, step)
        step *= 2

    def to_line(k):
        came = []
        for c in (0, 1):
            at = k * half + c * quarter
            under = jnp.pad(logs[at : at + quarter].reshape(1, quarter), ((0, PAD - 1), (0, depth - quarter)))
            part = jnp.concatenate([embed[at : at + quarter], under], axis=0)
            came.append(permute(part, [(ident(r, q // 2, q % 2), ident(q, r, c)) for q in rows for r in rows]))
        return jnp.where(core == 0, came[0], came[1])

    def along_line(part, after=()):
        step = groups // 2
        while step > 1:
            came = swapped(part, "col", 2 * step)
            part = part[: part.shape[0] - 2 * len(after)]
            part = jnp.concatenate([part, *[array[:2] for array in after], came], axis=0)
            after = ()
            step //= 2
        return part, swapped(part, "col", 2)

    under = jnp.pad(logs.reshape(share // depth, depth), ((0, PAD - share // depth), (0, 0)))
    coded = jnp.concatenate([embed, under], axis=0)
    pieces = {0: [coded]}
    layout = [(0, 0, share + PAD)]
    for m in range(1, groups):
        if m & (m - 1) == 0 or groups != 4:
            pieces[m] = [row_swapped(coded, m)]
            layout.append((m, 0, share + PAD))
    if groups == 4:
        pieces[3] = [row_swapped(pieces[2][0][:half], 1), row_swapped(pieces[1][0][half:], 2)]
        layout += [(3, 0, half), (3, half, half + PAD)]
    held = [pieces[m][start > 0] for m, start, _ in layout]

    part = to_line(0)
    part_row = lax.broadcasted_iota(jnp.int32, part.shape, 0)
    part = jnp.where(part_row == quarter + 1, plane_total[0, 0], part)
    for number, m in enumerate([1 << q for q in range(groups.bit_length() - 1)]):
        part = jnp.where(part_row == quarter + 2 + number, pieces[m][0][: quarter + PAD], part)
    lower, upper = along_line(part, pieces[3] if groups == 4 else ())
    vectors = [lower, upper, across(lower), across(upper)]

    listing = tile_list.reshape(-1)
    listed = jnp.sum((listing[None, :] == jnp.arange(listing.shape[0])[:, None]).astype(jnp.int32), axis=1)
    place = jnp.stack([g, chip, core]).astype(jnp.int32)

    def from_line_at_once(outs):
        summed = outs[0] + across(outs[1])
        parts = {d: summed[j * quarter : (j + 1) * quarter] for j, d in enumerate(order_of(groups))}
        total = parts[0]
        for d in range(1, groups):
            total = total + swapped(parts[d], "col", 2 * d)
        return summed, total

    def from_line(outs):
        summed = total = outs[0] + across(outs[1])
        step = 1
        while step < groups:
            kept = total.shape[0] // 2
            total = total[:kept] + swapped(total[kept:], "col", 2 * step)
            step *= 2
        return summed, total

    def to_home(total):
        homes = []
        for c in (0, 1):
            homes.append(permute(total, [(ident(q, r, c), ident(r, q // 2, q % 2)) for q in rows for r in rows]))
        return homes

    tiles = [(row, col) for row in range(groups * share // BLOCK) for col in range(groups * share // BLOCK)]
    grads = functools.partial(half_grads, groups=groups, share=share, layout=layout, place=place, listed=listed, cooc=cooc)
    lower, upper = along_line(to_line(1))
    outs = grads(0, tiles=tiles[:-1], vectors=vectors, held=held, row_in=None, ready=[lower])
    columns = outs[1:4]
    outs = grads(0, tiles=tiles[-1:], vectors=vectors, held=outs[1:], row_in=outs[0], ready=[upper])
    first_summed, first_total = from_line_at_once(outs)
    vectors = [lower, upper, across(lower), across(upper)]
    outs = grads(1, tiles=tiles[:-1], vectors=vectors, held=[*columns, outs[2]], row_in=None, ready=[first_summed])
    outs = grads(1, tiles=tiles[-1:], vectors=vectors, held=[*columns, outs[1]], row_in=outs[0], ready=[first_total])
    second_summed, second_total = from_line(outs)
    homes = to_home(jnp.concatenate([first_total, second_total], axis=0))
    quarters = [home[at : at + quarter] for at in (0, quarter) for home in homes]

    halves = outs[2:]
    if groups == 4:
        spare = second_summed[:PAD]
        first_x = row_swapped(jnp.concatenate([halves[2], halves[6], spare], axis=0), 1)[: 2 * half]
        first_y = row_swapped(jnp.concatenate([halves[5], halves[7], spare], axis=0), 2)[: 2 * half]
        second_x = row_swapped(halves[3] + first_y[half:], 1)
        second_y = row_swapped(halves[4] + first_x[half:], 2)
        top = halves[0] + first_x[:half] + second_y
        bottom = halves[1] + second_x + first_y[:half]
    else:
        top, bottom = halves[:2]
        for m in range(1, groups):
            top = top + row_swapped(halves[2 * m], m)
            bottom = bottom + row_swapped(halves[2 * m + 1], m)
    gradients = (jnp.concatenate([top, bottom], axis=0) + jnp.concatenate(quarters, axis=0)) / BLOCK
    new_accum = accum + gradients * gradients
    new_embed = embed - LEARN_RATE * gradients / jnp.sqrt(new_accum)
    return (new_embed, new_accum)


def solution(mesh):
    placed = (
        P("row", "col"),
        P("row", "col", None),
        P(("col", "row")),
        P(("col", "row"), None),
        P(("col", "row"), None),
    )
    return jax.shard_map(
        functools.partial(local, mesh.shape["row"], mesh.shape["col"]),
        mesh=mesh,
        in_specs=placed,
        out_specs=(P(("col", "row"), None), P(("col", "row"), None)),
        check_vma=False,
    )
```

```python
import functools

import jax
import jax.numpy as jnp
from jax import lax
from jax.experimental import pallas as pl
from jax.experimental.pallas import tpu as pltpu
from jax.sharding import PartitionSpec as P

BLOCK = 1024
LEARN_RATE = 0.05
SUB = 512
STEP = 128
PAD = 8
VMEM_LIMIT = 42 * 2**20


def split_bf16(values):
    high = values.astype(jnp.bfloat16)
    low = (values - high.astype(jnp.float32)).astype(jnp.bfloat16)
    return high, low


def product(left, right, dims):
    (left_at,), (right_at,) = dims
    left = jnp.concatenate([left[0], left[1], left[0]], axis=left_at)
    right = jnp.concatenate([right[0], right[0], right[1]], axis=right_at)
    return lax.dot_general(left, right, (dims, ((), ())), preferred_element_type=jnp.float32)


def order_of(count):
    order = [0]
    step = count // 2
    while step:
        order += [d + step for d in order]
        step //= 2
    return order


def half_kernel(k, groups, share, layout, tiles, first, added, ends, last, extra, *refs):
    rest = list(refs)
    take = lambda count: [rest.pop(0) for _ in range(count)]
    place_ref, listed_ref, cooc_ref = take(3)
    row_refs = take(4)
    order = order_of(groups)
    if first:
        pieces = take(len(layout))
    else:
        high_ref, low_ref, log_ref, sums_in = take(4)
    if added:
        (row_in,) = take(1)
    take(extra)
    if ends:
        mine_out, other_out = take(2)
    else:
        (row_out,) = take(1)
    if first:
        high_ref, low_ref, log_ref = take(3)
    if last:
        outs = take(2 * groups)
    else:
        (sums,) = take(1)
    row_vecs, row_logs, slope_high, slope_low, cells, cell_sems = take(6)
    if ends:
        (row_out,) = take(1)
    if last:
        (sums,) = take(1)

    depth = row_vecs.shape[1]
    half = share // 2
    quarter = share // 4
    cols = groups * share
    col_blocks = cols // BLOCK
    per = BLOCK // share
    tall = BLOCK // 2
    g = place_ref[0]
    chip = place_ref[1]
    core = place_ref[2]

    def cell_copies(row, col):
        number = tiles.index((row, col))
        return [
            pltpu.make_async_copy(
                cooc_ref.at[pl.ds((row * per + j) * share + k * half, half), pl.ds(col * BLOCK, BLOCK)],
                cells.at[number, pl.ds(j * half, half), :],
                cell_sems.at[number, j],
            )
            for j in range(per)
        ]

    for row, col in tiles:

        @pl.when(listed_ref[row * col_blocks + col] > 0)
        def _():
            for copy in cell_copies(row, col):
                copy.start()

    if first:
        total = jnp.zeros((1, 128), jnp.float32)
        for ref in row_refs:
            for j in range(groups // 2):
                at = j * (quarter + PAD) + quarter + 1
                total = total + ref[at : at + 1, :128]
        log_total = jnp.concatenate([jnp.log(total)] * (depth // 128), axis=1)
        for piece, (other, start, count) in zip(pieces, layout):
            body = min(count, share - start)
            at = pl.multiple_of((g ^ other) * share + start, 16)
            high, low = split_bf16(piece[:body, :])
            high_ref[pl.ds(at, body), :] = high
            low_ref[pl.ds(at, body), :] = low
            if body < count:
                at = pl.multiple_of((g ^ other) * PAD, PAD)
                log_ref[pl.ds(at, PAD), :] = piece[body:, :] - log_total
        sums[...] = jnp.zeros_like(sums)
    else:
        sums[...] = sums_in[...]

    for number, ref in enumerate(row_refs):
        side = core if number < 2 else 1 - core
        for j in range(groups // 2):
            d = order[number % 2 * (groups // 2) + j]
            start = j * (quarter + PAD)
            at = pl.multiple_of((chip ^ d) * half + side * quarter, quarter)
            row_vecs[pl.ds(at, quarter), :] = ref[start : start + quarter, :]
            log_row = ref[start + quarter : start + quarter + 1, :128]
            row_logs[pl.ds(at, quarter), :] = jnp.transpose(jnp.broadcast_to(log_row, (128, 128)))[:quarter, :]
    row_out[...] = row_in[...] if added else jnp.zeros_like(row_out)

    for row, col in tiles:
        tall_rows = slice(row * tall, (row + 1) * tall)

        @pl.when(listed_ref[row * col_blocks + col] > 0)
        def _():
            for copy in cell_copies(row, col):
                copy.wait()
            rows = row_vecs[tall_rows, :]
            row_high, row_low = split_bf16(rows)
            row_turned = split_bf16(jnp.transpose(rows))
            strips = BLOCK // SUB
            steps = [(strip, at) for strip in range(strips) for at in range(0, tall, STEP)]

            def col_pair(strip):
                at = col * BLOCK + strip * SUB
                return high_ref[at : at + SUB, :], low_ref[at : at + SUB, :]

            def scores(strip, at):
                pair = (row_high[at : at + STEP, :], row_low[at : at + STEP, :])
                return product(pair, col_pair(strip), ((1,), (1,)))

            def slopes(strip, at, values):
                col_at = col * BLOCK + strip * SUB
                log_rows = [
                    lane // share * PAD + lane % share // depth for lane in range(col_at, col_at + SUB, depth)
                ]
                col_log = jnp.concatenate([log_ref[q : q + 1, :] for q in log_rows], axis=1)
                row_log = row_logs[row * tall + at : row * tall + at + STEP, :]
                centred = values + jnp.concatenate([row_log] * (SUB // 128), axis=1) + col_log
                counts = cells[tiles.index((row, col)), at : at + STEP, strip * SUB : (strip + 1) * SUB]
                counts_f = counts.astype(jnp.float32)
                floor = jnp.maximum(counts_f, 1.0)
                weights = 0.1 + 0.25 * (counts_f * lax.rsqrt(floor))
                high, low = split_bf16(
                    jnp.where(
                        counts_f > 0,
                        weights * (centred - jnp.log(floor)),
                        0.5 * jnp.tanh(0.5 * centred) + 0.5,
                    )
                )
                slope_high[strip % 2, at : at + STEP, :] = high
                slope_low[strip % 2, at : at + STEP, :] = low
                return high, low

            def to_rows(strip, at, pair):
                row_out[row * tall + at : row * tall + at + STEP, :] += product(pair, col_pair(strip), ((1,), (0,)))

            def to_cols(strip):
                at = col * BLOCK + strip * SUB
                pair = (slope_high[strip % 2], slope_low[strip % 2])
                sums[:, at : at + SUB] += product(row_turned, pair, ((1,), (0,)))

            ahead = scores(*steps[0])
            behind = None
            for number, (strip, at) in enumerate(steps):
                values = ahead
                if number + 1 < len(steps):
                    ahead = scores(*steps[number + 1])
                if number > 0:
                    to_rows(*steps[number - 1], behind)
                if at == STEP and strip > 0:
                    to_cols(strip - 1)
                behind = slopes(strip, at, values)
            to_rows(*steps[-1], behind)
            to_cols(strips - 1)

    for out, side in ((mine_out, core), (other_out, 1 - core)) if ends else ():
        for j, d in enumerate(order):
            at = pl.multiple_of((chip ^ d) * half + side * quarter, quarter)
            out[j * quarter : (j + 1) * quarter, :] = row_out[pl.ds(at, quarter), :]
    if last:
        for other in range(groups):
            at = pl.multiple_of((g ^ other) * share, share)
            block = jnp.transpose(sums[:, pl.ds(at, share)])
            outs[2 * other][...] = block[:half]
            outs[2 * other + 1][...] = block[half:]


def half_grads(k, groups, share, layout, tiles, place, listed, cooc, vectors, held, row_in, ready):
    depth = vectors[0].shape[1]
    cols = groups * share
    first = k == 0 and tiles[0] == (0, 0)
    added = row_in is not None
    ends = tiles[-1] == (cols // BLOCK - 1,) * 2
    last = ends and k == 1
    per = BLOCK // share
    rows = groups * share // 2
    whole = pl.BlockSpec(memory_space=pltpu.VMEM)
    scalar = pl.BlockSpec(memory_space=pltpu.SMEM)
    remote = pl.BlockSpec(memory_space=pl.ANY)
    row_part = jax.ShapeDtypeStruct((rows // 2, depth), jnp.float32)
    row_all = jax.ShapeDtypeStruct((rows, depth), jnp.float32)
    col_half = jax.ShapeDtypeStruct((share // 2, depth), jnp.float32)
    coded = jax.ShapeDtypeStruct((cols, depth), jnp.bfloat16)
    logs = jax.ShapeDtypeStruct((groups * PAD, depth), jnp.float32)
    turned = jax.ShapeDtypeStruct((depth, cols), jnp.float32)
    out_shape = [row_part] * 2 if ends else [row_all]
    out_shape += [coded, coded, logs] if first else []
    out_shape += [col_half] * (2 * groups) if last else [turned]
    held = [*held, row_in] if added else [*held]
    args = [place, listed, cooc, *vectors, *held, *ready]
    in_specs = [scalar] * 2 + [remote] + [whole] * (4 + len(held)) + [remote] * len(ready)
    scratch = [
        pltpu.VMEM((rows, depth), jnp.float32),
        pltpu.VMEM((rows, 128), jnp.float32),
        pltpu.VMEM((2, BLOCK // 2, SUB), jnp.bfloat16),
        pltpu.VMEM((2, BLOCK // 2, SUB), jnp.bfloat16),
        pltpu.VMEM((len(tiles), BLOCK // 2, BLOCK), jnp.int32),
        pltpu.SemaphoreType.DMA((len(tiles), per)),
    ]
    if ends:
        scratch.append(pltpu.VMEM((rows, depth), jnp.float32))
    if last:
        scratch.append(pltpu.VMEM((depth, cols), jnp.float32))
    cells = len(tiles) * BLOCK * BLOCK // 2
    return pl.pallas_call(
        functools.partial(half_kernel, k, groups, share, layout, tiles, first, added, ends, last, len(ready)),
        out_shape=out_shape,
        in_specs=in_specs,
        out_specs=[whole] * len(out_shape),
        scratch_shapes=scratch,
        compiler_params=pltpu.CompilerParams(vmem_limit_bytes=VMEM_LIMIT),
        cost_estimate=pl.CostEstimate(
            flops=cells * depth * 18, bytes_accessed=4 * cells + 8 * cols * depth, transcendentals=3 * cells
        ),
        name="half_grads",
    )(*args)


def local(groups, col_groups, cooc, tile_list, marginal, embed, accum):
    assert col_groups == 2 * groups and groups & (groups - 1) == 0
    both = ("row", "col")
    g = lax.axis_index("row")
    h = lax.axis_index("col")
    chip = h // 2
    core = h % 2
    share, depth = embed.shape
    half = share // 2
    quarter = share // 4
    rows = range(groups)

    def ident(row, at, core):
        return row * col_groups + at * 2 + core

    def permute(value, pairs):
        return lax.ppermute(value, both, pairs)

    def swapped(value, axis, m):
        return lax.ppermute(value, axis, [(r, r ^ m) for r in range(lax.axis_size(axis))])

    def row_swapped(value, m):
        return swapped(value, "row", m)

    def across(value):
        return swapped(value, "col", 1)

    marg_f = marginal.astype(jnp.float32)
    logs = jnp.log(marg_f)

    plane_total = jnp.broadcast_to(jnp.sum(marg_f), (8, 128))
    step = 1
    while step < groups:
        plane_total = plane_total + row_swapped(plane_total, step)
        step *= 2

    def to_line(k):
        came = []
        for c in (0, 1):
            at = k * half + c * quarter
            under = jnp.pad(logs[at : at + quarter].reshape(1, quarter), ((0, PAD - 1), (0, depth - quarter)))
            part = jnp.concatenate([embed[at : at + quarter], under], axis=0)
            came.append(permute(part, [(ident(r, q // 2, q % 2), ident(q, r, c)) for q in rows for r in rows]))
        return jnp.where(core == 0, came[0], came[1])

    def along_line(part, after=()):
        step = groups // 2
        while step > 1:
            came = swapped(part, "col", 2 * step)
            part = part[: part.shape[0] - 2 * len(after)]
            part = jnp.concatenate([part, *[array[:2] for array in after], came], axis=0)
            after = ()
            step //= 2
        return part, swapped(part, "col", 2)

    under = jnp.pad(logs.reshape(share // depth, depth), ((0, PAD - share // depth), (0, 0)))
    coded = jnp.concatenate([embed, under], axis=0)
    pieces = {0: [coded]}
    layout = [(0, 0, share + PAD)]
    for m in range(1, groups):
        if m & (m - 1) == 0 or groups != 4:
            pieces[m] = [row_swapped(coded, m)]
            layout.append((m, 0, share + PAD))
    if groups == 4:
        pieces[3] = [row_swapped(pieces[2][0][:half], 1), row_swapped(pieces[1][0][half:], 2)]
        layout += [(3, 0, half), (3, half, half + PAD)]
    held = [pieces[m][start > 0] for m, start, _ in layout]

    part = to_line(0)
    part_row = lax.broadcasted_iota(jnp.int32, part.shape, 0)
    part = jnp.where(part_row == quarter + 1, plane_total[0, 0], part)
    for number, m in enumerate([1 << q for q in range(groups.bit_length() - 1)]):
        part = jnp.where(part_row == quarter + 2 + number, pieces[m][0][: quarter + PAD], part)
    lower, upper = along_line(part, pieces[3] if groups == 4 else ())
    vectors = [lower, upper, across(lower), across(upper)]

    listing = tile_list.reshape(-1)
    listed = jnp.sum((listing[None, :] == jnp.arange(listing.shape[0])[:, None]).astype(jnp.int32), axis=1)
    place = jnp.stack([g, chip, core]).astype(jnp.int32)

    def from_line_at_once(outs):
        summed = outs[0] + across(outs[1])
        parts = {d: summed[j * quarter : (j + 1) * quarter] for j, d in enumerate(order_of(groups))}
        total = parts[0]
        for d in range(1, groups):
            total = total + swapped(parts[d], "col", 2 * d)
        return summed, total

    def from_line(outs):
        summed = total = outs[0] + across(outs[1])
        step = 1
        while step < groups:
            kept = total.shape[0] // 2
            total = total[:kept] + swapped(total[kept:], "col", 2 * step)
            step *= 2
        return summed, total

    def to_home(total):
        homes = []
        for c in (0, 1):
            homes.append(permute(total, [(ident(q, r, c), ident(r, q // 2, q % 2)) for q in rows for r in rows]))
        return homes

    tiles = [(row, col) for row in range(groups * share // BLOCK) for col in range(groups * share // BLOCK)]
    grads = functools.partial(half_grads, groups=groups, share=share, layout=layout, place=place, listed=listed, cooc=cooc)
    lower, upper = along_line(to_line(1))
    outs = grads(0, tiles=tiles[:-1], vectors=vectors, held=held, row_in=None, ready=[lower])
    columns = outs[1:4]
    outs = grads(0, tiles=tiles[-1:], vectors=vectors, held=outs[1:], row_in=outs[0], ready=[upper])
    first_summed, first_total = from_line_at_once(outs)
    vectors = [lower, upper, across(lower), across(upper)]
    outs = grads(1, tiles=tiles[:-1], vectors=vectors, held=[*columns, outs[2]], row_in=None, ready=[first_summed])
    outs = grads(1, tiles=tiles[-1:], vectors=vectors, held=[*columns, outs[1]], row_in=outs[0], ready=[first_total])
    second_summed, second_total = from_line(outs)
    halves = outs[2:]
    if groups == 4:
        spare = second_summed[:PAD]
        first_x = row_swapped(jnp.concatenate([halves[2], halves[6], spare], axis=0), 1)[: 2 * half]
        first_y = row_swapped(jnp.concatenate([halves[5], halves[7], spare], axis=0), 2)[: 2 * half]
        waited = [first_x[:PAD], first_y[:PAD]]
        second_x = row_swapped(halves[3] + first_y[half:], 1)
        second_y = row_swapped(halves[4] + first_x[half:], 2)
        top = halves[0] + first_x[:half] + second_y
        bottom = halves[1] + second_x + first_y[:half]
    else:
        top, bottom = halves[:2]
        for m in range(1, groups):
            top = top + row_swapped(halves[2 * m], m)
            bottom = bottom + row_swapped(halves[2 * m + 1], m)
        waited = []
    homes = to_home(jnp.concatenate([first_total, second_total, *waited], axis=0))
    quarters = [home[at : at + quarter] for at in (0, quarter) for home in homes]
    gradients = (jnp.concatenate([top, bottom], axis=0) + jnp.concatenate(quarters, axis=0)) / BLOCK
    new_accum = accum + gradients * gradients
    new_embed = embed - LEARN_RATE * gradients / jnp.sqrt(new_accum)
    return (new_embed, new_accum)


def solution(mesh):
    placed = (
        P("row", "col"),
        P("row", "col", None),
        P(("col", "row")),
        P(("col", "row"), None),
        P(("col", "row"), None),
    )
    return jax.shard_map(
        functools.partial(local, mesh.shape["row"], mesh.shape["col"]),
        mesh=mesh,
        in_specs=placed,
        out_specs=(P(("col", "row"), None), P(("col", "row"), None)),
        check_vma=False,
    )
```

```python
import functools

import jax
import jax.numpy as jnp
from jax import lax
from jax.experimental import pallas as pl
from jax.experimental.pallas import tpu as pltpu
from jax.sharding import PartitionSpec as P

BLOCK = 1024
LEARN_RATE = 0.05
SUB = 512
PAD = 8
VMEM_LIMIT = 42 * 2**20


def split_bf16(values):
    high = values.astype(jnp.bfloat16)
    low = (values - high.astype(jnp.float32)).astype(jnp.bfloat16)
    return high, low


def product(left, right, dims):
    (left_at,), (right_at,) = dims
    left = jnp.concatenate([left[0], left[1], left[0]], axis=left_at)
    right = jnp.concatenate([right[0], right[0], right[1]], axis=right_at)
    return lax.dot_general(left, right, (dims, ((), ())), preferred_element_type=jnp.float32)


def order_of(count):
    order = [0]
    step = count // 2
    while step:
        order += [d + step for d in order]
        step //= 2
    return order


def half_kernel(k, groups, share, layout, tiles, first, added, ends, last, extra, *refs):
    rest = list(refs)
    take = lambda count: [rest.pop(0) for _ in range(count)]
    place_ref, listed_ref, cooc_ref = take(3)
    row_refs = take(4)
    order = order_of(groups)
    if first:
        pieces = take(len(layout))
    else:
        high_ref, low_ref, log_ref, sums_in = take(4)
    if added:
        (row_in,) = take(1)
    take(extra)
    if ends:
        mine_out, other_out = take(2)
    else:
        (row_out,) = take(1)
    if first:
        high_ref, low_ref, log_ref = take(3)
    if last:
        outs = take(2 * groups)
    else:
        (sums,) = take(1)
    row_vecs, row_logs, cells, cell_sems = take(4)
    if ends:
        (row_out,) = take(1)
    if last:
        (sums,) = take(1)

    depth = row_vecs.shape[1]
    half = share // 2
    quarter = share // 4
    cols = groups * share
    col_blocks = cols // BLOCK
    per = BLOCK // share
    tall = BLOCK // 2
    g = place_ref[0]
    chip = place_ref[1]
    core = place_ref[2]

    def cell_copies(row, col):
        number = tiles.index((row, col))
        return [
            pltpu.make_async_copy(
                cooc_ref.at[pl.ds((row * per + j) * share + k * half, half), pl.ds(col * BLOCK, BLOCK)],
                cells.at[number, pl.ds(j * half, half), :],
                cell_sems.at[number, j],
            )
            for j in range(per)
        ]

    for row, col in tiles:

        @pl.when(listed_ref[row * col_blocks + col] > 0)
        def _():
            for copy in cell_copies(row, col):
                copy.start()

    if first:
        total = jnp.zeros((1, 128), jnp.float32)
        for ref in row_refs:
            for j in range(groups // 2):
                at = j * (quarter + PAD) + quarter + 1
                total = total + ref[at : at + 1, :128]
        log_total = jnp.concatenate([jnp.log(total)] * (depth // 128), axis=1)
        for piece, (other, start, count) in zip(pieces, layout):
            body = min(count, share - start)
            at = pl.multiple_of((g ^ other) * share + start, 16)
            high, low = split_bf16(piece[:body, :])
            high_ref[pl.ds(at, body), :] = high
            low_ref[pl.ds(at, body), :] = low
            if body < count:
                at = pl.multiple_of((g ^ other) * PAD, PAD)
                log_ref[pl.ds(at, PAD), :] = piece[body:, :] - log_total
        sums[...] = jnp.zeros_like(sums)
    else:
        sums[...] = sums_in[...]

    for number, ref in enumerate(row_refs):
        side = core if number < 2 else 1 - core
        for j in range(groups // 2):
            d = order[number % 2 * (groups // 2) + j]
            start = j * (quarter + PAD)
            at = pl.multiple_of((chip ^ d) * half + side * quarter, quarter)
            row_vecs[pl.ds(at, quarter), :] = ref[start : start + quarter, :]
            log_row = ref[start + quarter : start + quarter + 1, :128]
            row_logs[pl.ds(at, quarter), :] = jnp.transpose(jnp.broadcast_to(log_row, (128, 128)))[:quarter, :]
    row_out[...] = row_in[...] if added else jnp.zeros_like(row_out)

    for row, col in tiles:
        tall_rows = slice(row * tall, (row + 1) * tall)

        @pl.when(listed_ref[row * col_blocks + col] > 0)
        def _():
            for copy in cell_copies(row, col):
                copy.wait()
            rows = row_vecs[tall_rows, :]
            row_pair = split_bf16(rows)
            row_turned = split_bf16(jnp.transpose(rows))
            row_log = jnp.concatenate([row_logs[tall_rows, :]] * (SUB // 128), axis=1)
            strips = BLOCK // SUB

            def col_pair(strip):
                at = col * BLOCK + strip * SUB
                return high_ref[at : at + SUB, :], low_ref[at : at + SUB, :]

            def scores(strip):
                return product(row_pair, col_pair(strip), ((1,), (1,)))

            def slopes(strip, values):
                at = col * BLOCK + strip * SUB
                log_rows = [lane // share * PAD + lane % share // depth for lane in range(at, at + SUB, depth)]
                col_log = jnp.concatenate([log_ref[q : q + 1, :] for q in log_rows], axis=1)
                centred = values + row_log + col_log
                counts = cells[tiles.index((row, col)), :, strip * SUB : (strip + 1) * SUB]
                counts_f = counts.astype(jnp.float32)
                floor = jnp.maximum(counts_f, 1.0)
                weights = 0.1 + 0.25 * (counts_f * lax.rsqrt(floor))
                return split_bf16(
                    jnp.where(
                        counts_f > 0,
                        weights * (centred - jnp.log(floor)),
                        0.5 * jnp.tanh(0.5 * centred) + 0.5,
                    )
                )

            def gradients(strip, pair):
                at = col * BLOCK + strip * SUB
                row_out[tall_rows, :] += product(pair, col_pair(strip), ((1,), (0,)))
                sums[:, at : at + SUB] += product(row_turned, pair, ((1,), (0,)))

            ahead = scores(0)
            behind = None
            for strip in range(strips):
                values = ahead
                if strip + 1 < strips:
                    ahead = scores(strip + 1)
                if strip > 0:
                    gradients(strip - 1, behind)
                behind = slopes(strip, values)
            gradients(strips - 1, behind)

    for out, side in ((mine_out, core), (other_out, 1 - core)) if ends else ():
        for j, d in enumerate(order):
            at = pl.multiple_of((chip ^ d) * half + side * quarter, quarter)
            out[j * quarter : (j + 1) * quarter, :] = row_out[pl.ds(at, quarter), :]
    if last:
        for other in range(groups):
            at = pl.multiple_of((g ^ other) * share, share)
            block = jnp.transpose(sums[:, pl.ds(at, share)])
            outs[2 * other][...] = block[:half]
            outs[2 * other + 1][...] = block[half:]


def half_grads(k, groups, share, layout, tiles, place, listed, cooc, vectors, held, row_in, ready):
    depth = vectors[0].shape[1]
    cols = groups * share
    first = k == 0 and tiles[0] == (0, 0)
    added = row_in is not None
    ends = tiles[-1] == (cols // BLOCK - 1,) * 2
    last = ends and k == 1
    per = BLOCK // share
    rows = groups * share // 2
    whole = pl.BlockSpec(memory_space=pltpu.VMEM)
    scalar = pl.BlockSpec(memory_space=pltpu.SMEM)
    remote = pl.BlockSpec(memory_space=pl.ANY)
    row_part = jax.ShapeDtypeStruct((rows // 2, depth), jnp.float32)
    row_all = jax.ShapeDtypeStruct((rows, depth), jnp.float32)
    col_half = jax.ShapeDtypeStruct((share // 2, depth), jnp.float32)
    coded = jax.ShapeDtypeStruct((cols, depth), jnp.bfloat16)
    logs = jax.ShapeDtypeStruct((groups * PAD, depth), jnp.float32)
    turned = jax.ShapeDtypeStruct((depth, cols), jnp.float32)
    out_shape = [row_part] * 2 if ends else [row_all]
    out_shape += [coded, coded, logs] if first else []
    out_shape += [col_half] * (2 * groups) if last else [turned]
    held = [*held, row_in] if added else [*held]
    args = [place, listed, cooc, *vectors, *held, *ready]
    in_specs = [scalar] * 2 + [remote] + [whole] * (4 + len(held)) + [remote] * len(ready)
    scratch = [
        pltpu.VMEM((rows, depth), jnp.float32),
        pltpu.VMEM((rows, 128), jnp.float32),
        pltpu.VMEM((len(tiles), BLOCK // 2, BLOCK), jnp.int32),
        pltpu.SemaphoreType.DMA((len(tiles), per)),
    ]
    if ends:
        scratch.append(pltpu.VMEM((rows, depth), jnp.float32))
    if last:
        scratch.append(pltpu.VMEM((depth, cols), jnp.float32))
    cells = len(tiles) * BLOCK * BLOCK // 2
    return pl.pallas_call(
        functools.partial(half_kernel, k, groups, share, layout, tiles, first, added, ends, last, len(ready)),
        out_shape=out_shape,
        in_specs=in_specs,
        out_specs=[whole] * len(out_shape),
        scratch_shapes=scratch,
        compiler_params=pltpu.CompilerParams(vmem_limit_bytes=VMEM_LIMIT),
        cost_estimate=pl.CostEstimate(
            flops=cells * depth * 18, bytes_accessed=4 * cells + 8 * cols * depth, transcendentals=3 * cells
        ),
        name="half_grads",
    )(*args)


def local(groups, col_groups, cooc, tile_list, marginal, embed, accum):
    assert col_groups == 2 * groups and groups & (groups - 1) == 0
    both = ("row", "col")
    g = lax.axis_index("row")
    h = lax.axis_index("col")
    chip = h // 2
    core = h % 2
    share, depth = embed.shape
    half = share // 2
    quarter = share // 4
    rows = range(groups)

    def ident(row, at, core):
        return row * col_groups + at * 2 + core

    def permute(value, pairs):
        return lax.ppermute(value, both, pairs)

    def swapped(value, axis, m):
        return lax.ppermute(value, axis, [(r, r ^ m) for r in range(lax.axis_size(axis))])

    def row_swapped(value, m):
        return swapped(value, "row", m)

    def across(value):
        return swapped(value, "col", 1)

    marg_f = marginal.astype(jnp.float32)
    logs = jnp.log(marg_f)

    plane_total = jnp.broadcast_to(jnp.sum(marg_f), (8, 128))
    step = 1
    while step < groups:
        plane_total = plane_total + row_swapped(plane_total, step)
        step *= 2

    def to_line(k):
        came = []
        for c in (0, 1):
            at = k * half + c * quarter
            under = jnp.pad(logs[at : at + quarter].reshape(1, quarter), ((0, PAD - 1), (0, depth - quarter)))
            part = jnp.concatenate([embed[at : at + quarter], under], axis=0)
            came.append(permute(part, [(ident(r, q // 2, q % 2), ident(q, r, c)) for q in rows for r in rows]))
        return jnp.where(core == 0, came[0], came[1])

    def along_line(part, after=()):
        step = groups // 2
        while step > 1:
            came = swapped(part, "col", 2 * step)
            part = part[: part.shape[0] - 2 * len(after)]
            part = jnp.concatenate([part, *[array[:2] for array in after], came], axis=0)
            after = ()
            step //= 2
        return part, swapped(part, "col", 2)

    under = jnp.pad(logs.reshape(share // depth, depth), ((0, PAD - share // depth), (0, 0)))
    coded = jnp.concatenate([embed, under], axis=0)
    pieces = {0: [coded]}
    layout = [(0, 0, share + PAD)]
    for m in range(1, groups):
        if m & (m - 1) == 0 or groups != 4:
            pieces[m] = [row_swapped(coded, m)]
            layout.append((m, 0, share + PAD))
    if groups == 4:
        pieces[3] = [row_swapped(pieces[2][0][:half], 1), row_swapped(pieces[1][0][half:], 2)]
        layout += [(3, 0, half), (3, half, half + PAD)]
    held = [pieces[m][start > 0] for m, start, _ in layout]

    part = to_line(0)
    part_row = lax.broadcasted_iota(jnp.int32, part.shape, 0)
    part = jnp.where(part_row == quarter + 1, plane_total[0, 0], part)
    for number, m in enumerate([1 << q for q in range(groups.bit_length() - 1)]):
        part = jnp.where(part_row == quarter + 2 + number, pieces[m][0][: quarter + PAD], part)
    lower, upper = along_line(part, pieces[3] if groups == 4 else ())
    vectors = [lower, upper, across(lower), across(upper)]

    listing = tile_list.reshape(-1)
    listed = jnp.sum((listing[None, :] == jnp.arange(listing.shape[0])[:, None]).astype(jnp.int32), axis=1)
    place = jnp.stack([g, chip, core]).astype(jnp.int32)

    def from_line(outs):
        summed = outs[0] + across(outs[1])
        parts = {d: summed[j * quarter : (j + 1) * quarter] for j, d in enumerate(order_of(groups))}
        total = parts[0]
        for d in range(1, groups):
            total = total + swapped(parts[d], "col", 2 * d)
        return summed, total

    def to_home(total):
        homes = []
        for c in (0, 1):
            homes.append(permute(total, [(ident(q, r, c), ident(r, q // 2, q % 2)) for q in rows for r in rows]))
        return homes

    tiles = [(row, col) for row in range(groups * share // BLOCK) for col in range(groups * share // BLOCK)]
    grads = functools.partial(half_grads, groups=groups, share=share, layout=layout, place=place, listed=listed, cooc=cooc)
    lower, upper = along_line(to_line(1))
    outs = grads(0, tiles=tiles[:-1], vectors=vectors, held=held, row_in=None, ready=[lower])
    columns = outs[1:4]
    outs = grads(0, tiles=tiles[-1:], vectors=vectors, held=outs[1:], row_in=outs[0], ready=[upper])
    first_summed, first_total = from_line(outs)
    vectors = [lower, upper, across(lower), across(upper)]
    outs = grads(1, tiles=tiles[:-1], vectors=vectors, held=[*columns, outs[2]], row_in=None, ready=[first_summed])
    outs = grads(1, tiles=tiles[-1:], vectors=vectors, held=[*columns, outs[1]], row_in=outs[0], ready=[first_total])
    second_summed, second_total = from_line(outs)
    halves = outs[2:]
    if groups == 4:
        spare = second_summed[:PAD]
        first_x = row_swapped(jnp.concatenate([halves[2], halves[6], spare], axis=0), 1)[: 2 * half]
        first_y = row_swapped(jnp.concatenate([halves[5], halves[7], spare], axis=0), 2)[: 2 * half]
        waited = [first_x[:PAD], first_y[:PAD]]
        second_x = row_swapped(halves[3] + first_y[half:], 1)
        second_y = row_swapped(halves[4] + first_x[half:], 2)
        top = halves[0] + first_x[:half] + second_y
        bottom = halves[1] + second_x + first_y[:half]
    else:
        top, bottom = halves[:2]
        for m in range(1, groups):
            top = top + row_swapped(halves[2 * m], m)
            bottom = bottom + row_swapped(halves[2 * m + 1], m)
        waited = []
    homes = to_home(jnp.concatenate([first_total, second_total, *waited], axis=0))
    quarters = [home[at : at + quarter] for at in (0, quarter) for home in homes]
    gradients = (jnp.concatenate([top, bottom], axis=0) + jnp.concatenate(quarters, axis=0)) / BLOCK
    new_accum = accum + gradients * gradients
    new_embed = embed - LEARN_RATE * gradients / jnp.sqrt(new_accum)
    return (new_embed, new_accum)


def solution(mesh):
    placed = (
        P("row", "col"),
        P("row", "col", None),
        P(("col", "row")),
        P(("col", "row"), None),
        P(("col", "row"), None),
    )
    return jax.shard_map(
        functools.partial(local, mesh.shape["row"], mesh.shape["col"]),
        mesh=mesh,
        in_specs=placed,
        out_specs=(P(("col", "row"), None), P(("col", "row"), None)),
        check_vma=False,
    )
```

```python
import functools

import jax
import jax.numpy as jnp
from jax import lax
from jax.experimental import pallas as pl
from jax.experimental.pallas import tpu as pltpu
from jax.sharding import PartitionSpec as P

BLOCK = 1024
LEARN_RATE = 0.05
SUB = 1024
PAD = 8
VMEM_LIMIT = 42 * 2**20


def split_bf16(values):
    high = values.astype(jnp.bfloat16)
    low = (values - high.astype(jnp.float32)).astype(jnp.bfloat16)
    return high, low


def product(left, right, dims):
    (left_at,), (right_at,) = dims
    left = jnp.concatenate([left[0], left[1], left[0]], axis=left_at)
    right = jnp.concatenate([right[0], right[0], right[1]], axis=right_at)
    return lax.dot_general(left, right, (dims, ((), ())), preferred_element_type=jnp.float32)


def order_of(count):
    order = [0]
    step = count // 2
    while step:
        order += [d + step for d in order]
        step //= 2
    return order


def half_kernel(k, groups, share, layout, tiles, first, added, ends, last, extra, *refs):
    rest = list(refs)
    take = lambda count: [rest.pop(0) for _ in range(count)]
    place_ref, listed_ref, cooc_ref = take(3)
    row_refs = take(4)
    order = order_of(groups)
    if first:
        pieces = take(len(layout))
    else:
        high_ref, low_ref, log_ref, sums_in = take(4)
    if added:
        (row_in,) = take(1)
    take(extra)
    if ends:
        mine_out, other_out = take(2)
    else:
        (row_out,) = take(1)
    if first:
        high_ref, low_ref, log_ref = take(3)
    if last:
        outs = take(2 * groups)
    else:
        (sums,) = take(1)
    row_vecs, row_logs, cells, cell_sems = take(4)
    if ends:
        (row_out,) = take(1)
    if last:
        (sums,) = take(1)

    depth = row_vecs.shape[1]
    half = share // 2
    quarter = share // 4
    cols = groups * share
    col_blocks = cols // BLOCK
    per = BLOCK // share
    tall = BLOCK // 2
    g = place_ref[0]
    chip = place_ref[1]
    core = place_ref[2]

    def cell_copies(row, col):
        number = tiles.index((row, col))
        return [
            pltpu.make_async_copy(
                cooc_ref.at[pl.ds((row * per + j) * share + k * half, half), pl.ds(col * BLOCK, BLOCK)],
                cells.at[number, pl.ds(j * half, half), :],
                cell_sems.at[number, j],
            )
            for j in range(per)
        ]

    for row, col in tiles:

        @pl.when(listed_ref[row * col_blocks + col] > 0)
        def _():
            for copy in cell_copies(row, col):
                copy.start()

    if first:
        total = jnp.zeros((1, 128), jnp.float32)
        for ref in row_refs:
            for j in range(groups // 2):
                at = j * (quarter + PAD) + quarter + 1
                total = total + ref[at : at + 1, :128]
        log_total = jnp.concatenate([jnp.log(total)] * (depth // 128), axis=1)
        for piece, (other, start, count) in zip(pieces, layout):
            body = min(count, share - start)
            at = pl.multiple_of((g ^ other) * share + start, 16)
            high, low = split_bf16(piece[:body, :])
            high_ref[pl.ds(at, body), :] = high
            low_ref[pl.ds(at, body), :] = low
            if body < count:
                at = pl.multiple_of((g ^ other) * PAD, PAD)
                log_ref[pl.ds(at, PAD), :] = piece[body:, :] - log_total
        sums[...] = jnp.zeros_like(sums)
    else:
        sums[...] = sums_in[...]

    for number, ref in enumerate(row_refs):
        side = core if number < 2 else 1 - core
        for j in range(groups // 2):
            d = order[number % 2 * (groups // 2) + j]
            start = j * (quarter + PAD)
            at = pl.multiple_of((chip ^ d) * half + side * quarter, quarter)
            row_vecs[pl.ds(at, quarter), :] = ref[start : start + quarter, :]
            log_row = ref[start + quarter : start + quarter + 1, :128]
            row_logs[pl.ds(at, quarter), :] = jnp.transpose(jnp.broadcast_to(log_row, (128, 128)))[:quarter, :]
    row_out[...] = row_in[...] if added else jnp.zeros_like(row_out)

    for row, col in tiles:
        tall_rows = slice(row * tall, (row + 1) * tall)

        @pl.when(listed_ref[row * col_blocks + col] > 0)
        def _():
            for copy in cell_copies(row, col):
                copy.wait()
            rows = row_vecs[tall_rows, :]
            row_pair = split_bf16(rows)
            row_turned = split_bf16(jnp.transpose(rows))
            row_log = jnp.concatenate([row_logs[tall_rows, :]] * (SUB // 128), axis=1)
            strips = BLOCK // SUB

            def col_pair(strip):
                at = col * BLOCK + strip * SUB
                return high_ref[at : at + SUB, :], low_ref[at : at + SUB, :]

            def scores(strip):
                return product(row_pair, col_pair(strip), ((1,), (1,)))

            def slopes(strip, values):
                at = col * BLOCK + strip * SUB
                log_rows = [lane // share * PAD + lane % share // depth for lane in range(at, at + SUB, depth)]
                col_log = jnp.concatenate([log_ref[q : q + 1, :] for q in log_rows], axis=1)
                centred = values + row_log + col_log
                counts = cells[tiles.index((row, col)), :, strip * SUB : (strip + 1) * SUB]
                counts_f = counts.astype(jnp.float32)
                floor = jnp.maximum(counts_f, 1.0)
                weights = 0.1 + 0.25 * (counts_f * lax.rsqrt(floor))
                return split_bf16(
                    jnp.where(
                        counts_f > 0,
                        weights * (centred - jnp.log(floor)),
                        0.5 * jnp.tanh(0.5 * centred) + 0.5,
                    )
                )

            def gradients(strip, pair):
                at = col * BLOCK + strip * SUB
                row_out[tall_rows, :] += product(pair, col_pair(strip), ((1,), (0,)))
                sums[:, at : at + SUB] += product(row_turned, pair, ((1,), (0,)))

            ahead = scores(0)
            behind = None
            for strip in range(strips):
                values = ahead
                if strip + 1 < strips:
                    ahead = scores(strip + 1)
                if strip > 0:
                    gradients(strip - 1, behind)
                behind = slopes(strip, values)
            gradients(strips - 1, behind)

    for out, side in ((mine_out, core), (other_out, 1 - core)) if ends else ():
        for j, d in enumerate(order):
            at = pl.multiple_of((chip ^ d) * half + side * quarter, quarter)
            out[j * quarter : (j + 1) * quarter, :] = row_out[pl.ds(at, quarter), :]
    if last:
        for other in range(groups):
            at = pl.multiple_of((g ^ other) * share, share)
            block = jnp.transpose(sums[:, pl.ds(at, share)])
            outs[2 * other][...] = block[:half]
            outs[2 * other + 1][...] = block[half:]


def half_grads(k, groups, share, layout, tiles, place, listed, cooc, vectors, held, row_in, ready):
    depth = vectors[0].shape[1]
    cols = groups * share
    first = k == 0 and tiles[0] == (0, 0)
    added = row_in is not None
    ends = tiles[-1] == (cols // BLOCK - 1,) * 2
    last = ends and k == 1
    per = BLOCK // share
    rows = groups * share // 2
    whole = pl.BlockSpec(memory_space=pltpu.VMEM)
    scalar = pl.BlockSpec(memory_space=pltpu.SMEM)
    remote = pl.BlockSpec(memory_space=pl.ANY)
    row_part = jax.ShapeDtypeStruct((rows // 2, depth), jnp.float32)
    row_all = jax.ShapeDtypeStruct((rows, depth), jnp.float32)
    col_half = jax.ShapeDtypeStruct((share // 2, depth), jnp.float32)
    coded = jax.ShapeDtypeStruct((cols, depth), jnp.bfloat16)
    logs = jax.ShapeDtypeStruct((groups * PAD, depth), jnp.float32)
    turned = jax.ShapeDtypeStruct((depth, cols), jnp.float32)
    out_shape = [row_part] * 2 if ends else [row_all]
    out_shape += [coded, coded, logs] if first else []
    out_shape += [col_half] * (2 * groups) if last else [turned]
    held = [*held, row_in] if added else [*held]
    args = [place, listed, cooc, *vectors, *held, *ready]
    in_specs = [scalar] * 2 + [remote] + [whole] * (4 + len(held)) + [remote] * len(ready)
    scratch = [
        pltpu.VMEM((rows, depth), jnp.float32),
        pltpu.VMEM((rows, 128), jnp.float32),
        pltpu.VMEM((len(tiles), BLOCK // 2, BLOCK), jnp.int32),
        pltpu.SemaphoreType.DMA((len(tiles), per)),
    ]
    if ends:
        scratch.append(pltpu.VMEM((rows, depth), jnp.float32))
    if last:
        scratch.append(pltpu.VMEM((depth, cols), jnp.float32))
    cells = len(tiles) * BLOCK * BLOCK // 2
    return pl.pallas_call(
        functools.partial(half_kernel, k, groups, share, layout, tiles, first, added, ends, last, len(ready)),
        out_shape=out_shape,
        in_specs=in_specs,
        out_specs=[whole] * len(out_shape),
        scratch_shapes=scratch,
        compiler_params=pltpu.CompilerParams(vmem_limit_bytes=VMEM_LIMIT),
        cost_estimate=pl.CostEstimate(
            flops=cells * depth * 18, bytes_accessed=4 * cells + 8 * cols * depth, transcendentals=3 * cells
        ),
        name="half_grads",
    )(*args)


def local(groups, col_groups, cooc, tile_list, marginal, embed, accum):
    assert col_groups == 2 * groups and groups & (groups - 1) == 0
    both = ("row", "col")
    g = lax.axis_index("row")
    h = lax.axis_index("col")
    chip = h // 2
    core = h % 2
    share, depth = embed.shape
    half = share // 2
    quarter = share // 4
    rows = range(groups)

    def ident(row, at, core):
        return row * col_groups + at * 2 + core

    def permute(value, pairs):
        return lax.ppermute(value, both, pairs)

    def swapped(value, axis, m):
        return lax.ppermute(value, axis, [(r, r ^ m) for r in range(lax.axis_size(axis))])

    def row_swapped(value, m):
        return swapped(value, "row", m)

    def across(value):
        return swapped(value, "col", 1)

    marg_f = marginal.astype(jnp.float32)
    logs = jnp.log(marg_f)

    plane_total = jnp.broadcast_to(jnp.sum(marg_f), (8, 128))
    step = 1
    while step < groups:
        plane_total = plane_total + row_swapped(plane_total, step)
        step *= 2

    def to_line(k):
        came = []
        for c in (0, 1):
            at = k * half + c * quarter
            under = jnp.pad(logs[at : at + quarter].reshape(1, quarter), ((0, PAD - 1), (0, depth - quarter)))
            part = jnp.concatenate([embed[at : at + quarter], under], axis=0)
            came.append(permute(part, [(ident(r, q // 2, q % 2), ident(q, r, c)) for q in rows for r in rows]))
        return jnp.where(core == 0, came[0], came[1])

    def along_line(part, after=()):
        step = groups // 2
        while step > 1:
            came = swapped(part, "col", 2 * step)
            part = part[: part.shape[0] - 2 * len(after)]
            part = jnp.concatenate([part, *[array[:2] for array in after], came], axis=0)
            after = ()
            step //= 2
        return part, swapped(part, "col", 2)

    under = jnp.pad(logs.reshape(share // depth, depth), ((0, PAD - share // depth), (0, 0)))
    coded = jnp.concatenate([embed, under], axis=0)
    pieces = {0: [coded]}
    layout = [(0, 0, share + PAD)]
    for m in range(1, groups):
        if m & (m - 1) == 0 or groups != 4:
            pieces[m] = [row_swapped(coded, m)]
            layout.append((m, 0, share + PAD))
    if groups == 4:
        pieces[3] = [row_swapped(pieces[2][0][:half], 1), row_swapped(pieces[1][0][half:], 2)]
        layout += [(3, 0, half), (3, half, half + PAD)]
    held = [pieces[m][start > 0] for m, start, _ in layout]

    part = to_line(0)
    part_row = lax.broadcasted_iota(jnp.int32, part.shape, 0)
    part = jnp.where(part_row == quarter + 1, plane_total[0, 0], part)
    for number, m in enumerate([1 << q for q in range(groups.bit_length() - 1)]):
        part = jnp.where(part_row == quarter + 2 + number, pieces[m][0][: quarter + PAD], part)
    lower, upper = along_line(part, pieces[3] if groups == 4 else ())
    vectors = [lower, upper, across(lower), across(upper)]

    listing = tile_list.reshape(-1)
    listed = jnp.sum((listing[None, :] == jnp.arange(listing.shape[0])[:, None]).astype(jnp.int32), axis=1)
    place = jnp.stack([g, chip, core]).astype(jnp.int32)

    def from_line_at_once(outs):
        summed = outs[0] + across(outs[1])
        parts = {d: summed[j * quarter : (j + 1) * quarter] for j, d in enumerate(order_of(groups))}
        total = parts[0]
        for d in range(1, groups):
            total = total + swapped(parts[d], "col", 2 * d)
        return summed, total

    def from_line(outs):
        summed = total = outs[0] + across(outs[1])
        step = 1
        while step < groups:
            kept = total.shape[0] // 2
            total = total[:kept] + swapped(total[kept:], "col", 2 * step)
            step *= 2
        return summed, total

    def to_home(total):
        homes = []
        for c in (0, 1):
            homes.append(permute(total, [(ident(q, r, c), ident(r, q // 2, q % 2)) for q in rows for r in rows]))
        return homes

    tiles = [(row, col) for row in range(groups * share // BLOCK) for col in range(groups * share // BLOCK)]
    grads = functools.partial(half_grads, groups=groups, share=share, layout=layout, place=place, listed=listed, cooc=cooc)
    lower, upper = along_line(to_line(1))
    outs = grads(0, tiles=tiles[:-1], vectors=vectors, held=held, row_in=None, ready=[lower])
    columns = outs[1:4]
    outs = grads(0, tiles=tiles[-1:], vectors=vectors, held=outs[1:], row_in=outs[0], ready=[upper])
    first_summed, first_total = from_line_at_once(outs)
    vectors = [lower, upper, across(lower), across(upper)]
    outs = grads(1, tiles=tiles[:-1], vectors=vectors, held=[*columns, outs[2]], row_in=None, ready=[first_summed])
    outs = grads(1, tiles=tiles[-1:], vectors=vectors, held=[*columns, outs[1]], row_in=outs[0], ready=[first_total])
    second_summed, second_total = from_line(outs)
    first_quarters = to_home(first_total)
    quarters = first_quarters + to_home(second_total)

    halves = outs[2:]
    if groups == 4:
        spare = second_summed[:PAD] + first_quarters[0][:PAD] + first_quarters[1][:PAD]
        first_x = row_swapped(jnp.concatenate([halves[2], halves[6], spare], axis=0), 1)[: 2 * half]
        first_y = row_swapped(jnp.concatenate([halves[5], halves[7], spare], axis=0), 2)[: 2 * half]
        second_x = row_swapped(halves[3] + first_y[half:], 1)
        second_y = row_swapped(halves[4] + first_x[half:], 2)
        top = halves[0] + first_x[:half] + second_y
        bottom = halves[1] + second_x + first_y[:half]
    else:
        top, bottom = halves[:2]
        for m in range(1, groups):
            top = top + row_swapped(halves[2 * m], m)
            bottom = bottom + row_swapped(halves[2 * m + 1], m)
    gradients = (jnp.concatenate([top, bottom], axis=0) + jnp.concatenate(quarters, axis=0)) / BLOCK
    new_accum = accum + gradients * gradients
    new_embed = embed - LEARN_RATE * gradients / jnp.sqrt(new_accum)
    return (new_embed, new_accum)


def solution(mesh):
    placed = (
        P("row", "col"),
        P("row", "col", None),
        P(("col", "row")),
        P(("col", "row"), None),
        P(("col", "row"), None),
    )
    return jax.shard_map(
        functools.partial(local, mesh.shape["row"], mesh.shape["col"]),
        mesh=mesh,
        in_specs=placed,
        out_specs=(P(("col", "row"), None), P(("col", "row"), None)),
        check_vma=False,
    )
```

```python
import functools

import jax
import jax.numpy as jnp
from jax import lax
from jax.experimental import pallas as pl
from jax.experimental.pallas import tpu as pltpu
from jax.sharding import PartitionSpec as P

BLOCK = 1024
LEARN_RATE = 0.05
SUB = 1024
PAD = 8
VMEM_LIMIT = 42 * 2**20


def split_bf16(values):
    high = values.astype(jnp.bfloat16)
    low = (values - high.astype(jnp.float32)).astype(jnp.bfloat16)
    return high, low


def product(left, right, dims):
    (left_at,), (right_at,) = dims
    left = jnp.concatenate([left[0], left[1], left[0]], axis=left_at)
    right = jnp.concatenate([right[0], right[0], right[1]], axis=right_at)
    return lax.dot_general(left, right, (dims, ((), ())), preferred_element_type=jnp.float32)


def order_of(count):
    order = [0]
    step = count // 2
    while step:
        order += [d + step for d in order]
        step //= 2
    return order


def half_kernel(k, groups, share, layout, tiles, first, added, ends, last, extra, *refs):
    rest = list(refs)
    take = lambda count: [rest.pop(0) for _ in range(count)]
    place_ref, listed_ref, cooc_ref = take(3)
    row_refs = take(4)
    order = order_of(groups)
    if first:
        pieces = take(len(layout))
    else:
        high_ref, low_ref, log_ref, sums_in = take(4)
    if added:
        (row_in,) = take(1)
    take(extra)
    if ends:
        mine_out, other_out = take(2)
    else:
        (row_out,) = take(1)
    if first:
        high_ref, low_ref, log_ref = take(3)
    if last:
        outs = take(2 * groups)
    else:
        (sums,) = take(1)
    row_vecs, row_logs, cells, cell_sems = take(4)
    if ends:
        (row_out,) = take(1)
    if last:
        (sums,) = take(1)

    depth = row_vecs.shape[1]
    half = share // 2
    quarter = share // 4
    cols = groups * share
    col_blocks = cols // BLOCK
    per = BLOCK // share
    tall = BLOCK // 2
    g = place_ref[0]
    chip = place_ref[1]
    core = place_ref[2]

    def cell_copies(row, col):
        number = tiles.index((row, col))
        return [
            pltpu.make_async_copy(
                cooc_ref.at[pl.ds((row * per + j) * share + k * half, half), pl.ds(col * BLOCK, BLOCK)],
                cells.at[number, pl.ds(j * half, half), :],
                cell_sems.at[number, j],
            )
            for j in range(per)
        ]

    for row, col in tiles:

        @pl.when(listed_ref[row * col_blocks + col] > 0)
        def _():
            for copy in cell_copies(row, col):
                copy.start()

    if first:
        total = jnp.zeros((1, 128), jnp.float32)
        for ref in row_refs:
            for j in range(groups // 2):
                at = j * (quarter + PAD) + quarter + 1
                total = total + ref[at : at + 1, :128]
        log_total = jnp.concatenate([jnp.log(total)] * (depth // 128), axis=1)
        for piece, (other, start, count) in zip(pieces, layout):
            body = min(count, share - start)
            at = pl.multiple_of((g ^ other) * share + start, 16)
            high, low = split_bf16(piece[:body, :])
            high_ref[pl.ds(at, body), :] = high
            low_ref[pl.ds(at, body), :] = low
            if body < count:
                at = pl.multiple_of((g ^ other) * PAD, PAD)
                log_ref[pl.ds(at, PAD), :] = piece[body:, :] - log_total
        sums[...] = jnp.zeros_like(sums)
    else:
        sums[...] = sums_in[...]

    for number, ref in enumerate(row_refs):
        side = core if number < 2 else 1 - core
        for j in range(groups // 2):
            d = order[number % 2 * (groups // 2) + j]
            start = j * (quarter + PAD)
            at = pl.multiple_of((chip ^ d) * half + side * quarter, quarter)
            row_vecs[pl.ds(at, quarter), :] = ref[start : start + quarter, :]
            log_row = ref[start + quarter : start + quarter + 1, :128]
            row_logs[pl.ds(at, quarter), :] = jnp.transpose(jnp.broadcast_to(log_row, (128, 128)))[:quarter, :]
    row_out[...] = row_in[...] if added else jnp.zeros_like(row_out)

    for row, col in tiles:
        tall_rows = slice(row * tall, (row + 1) * tall)

        @pl.when(listed_ref[row * col_blocks + col] > 0)
        def _():
            for copy in cell_copies(row, col):
                copy.wait()
            rows = row_vecs[tall_rows, :]
            row_pair = split_bf16(rows)
            row_turned = split_bf16(jnp.transpose(rows))
            row_log = jnp.concatenate([row_logs[tall_rows, :]] * (SUB // 128), axis=1)
            strips = BLOCK // SUB

            def col_pair(strip):
                at = col * BLOCK + strip * SUB
                return high_ref[at : at + SUB, :], low_ref[at : at + SUB, :]

            def scores(strip):
                return product(row_pair, col_pair(strip), ((1,), (1,)))

            def slopes(strip, values):
                at = col * BLOCK + strip * SUB
                log_rows = [lane // share * PAD + lane % share // depth for lane in range(at, at + SUB, depth)]
                col_log = jnp.concatenate([log_ref[q : q + 1, :] for q in log_rows], axis=1)
                centred = values + row_log + col_log
                counts = cells[tiles.index((row, col)), :, strip * SUB : (strip + 1) * SUB]
                counts_f = counts.astype(jnp.float32)
                floor = jnp.maximum(counts_f, 1.0)
                weights = 0.1 + 0.25 * (counts_f * lax.rsqrt(floor))
                return split_bf16(
                    jnp.where(
                        counts_f > 0,
                        weights * (centred - jnp.log(floor)),
                        0.5 * jnp.tanh(0.5 * centred) + 0.5,
                    )
                )

            def gradients(strip, pair):
                at = col * BLOCK + strip * SUB
                row_out[tall_rows, :] += product(pair, col_pair(strip), ((1,), (0,)))
                sums[:, at : at + SUB] += product(row_turned, pair, ((1,), (0,)))

            ahead = scores(0)
            behind = None
            for strip in range(strips):
                values = ahead
                if strip + 1 < strips:
                    ahead = scores(strip + 1)
                if strip > 0:
                    gradients(strip - 1, behind)
                behind = slopes(strip, values)
            gradients(strips - 1, behind)

    for out, side in ((mine_out, core), (other_out, 1 - core)) if ends else ():
        for j, d in enumerate(order):
            at = pl.multiple_of((chip ^ d) * half + side * quarter, quarter)
            out[j * quarter : (j + 1) * quarter, :] = row_out[pl.ds(at, quarter), :]
    if last:
        for other in range(groups):
            at = pl.multiple_of((g ^ other) * share, share)
            block = jnp.transpose(sums[:, pl.ds(at, share)])
            outs[2 * other][...] = block[:half]
            outs[2 * other + 1][...] = block[half:]


def half_grads(k, groups, share, layout, tiles, place, listed, cooc, vectors, held, row_in, ready):
    depth = vectors[0].shape[1]
    cols = groups * share
    first = k == 0 and tiles[0] == (0, 0)
    added = row_in is not None
    ends = tiles[-1] == (cols // BLOCK - 1,) * 2
    last = ends and k == 1
    per = BLOCK // share
    rows = groups * share // 2
    whole = pl.BlockSpec(memory_space=pltpu.VMEM)
    scalar = pl.BlockSpec(memory_space=pltpu.SMEM)
    remote = pl.BlockSpec(memory_space=pl.ANY)
    row_part = jax.ShapeDtypeStruct((rows // 2, depth), jnp.float32)
    row_all = jax.ShapeDtypeStruct((rows, depth), jnp.float32)
    col_half = jax.ShapeDtypeStruct((share // 2, depth), jnp.float32)
    coded = jax.ShapeDtypeStruct((cols, depth), jnp.bfloat16)
    logs = jax.ShapeDtypeStruct((groups * PAD, depth), jnp.float32)
    turned = jax.ShapeDtypeStruct((depth, cols), jnp.float32)
    out_shape = [row_part] * 2 if ends else [row_all]
    out_shape += [coded, coded, logs] if first else []
    out_shape += [col_half] * (2 * groups) if last else [turned]
    held = [*held, row_in] if added else [*held]
    args = [place, listed, cooc, *vectors, *held, *ready]
    in_specs = [scalar] * 2 + [remote] + [whole] * (4 + len(held)) + [remote] * len(ready)
    scratch = [
        pltpu.VMEM((rows, depth), jnp.float32),
        pltpu.VMEM((rows, 128), jnp.float32),
        pltpu.VMEM((len(tiles), BLOCK // 2, BLOCK), jnp.int32),
        pltpu.SemaphoreType.DMA((len(tiles), per)),
    ]
    if ends:
        scratch.append(pltpu.VMEM((rows, depth), jnp.float32))
    if last:
        scratch.append(pltpu.VMEM((depth, cols), jnp.float32))
    cells = len(tiles) * BLOCK * BLOCK // 2
    return pl.pallas_call(
        functools.partial(half_kernel, k, groups, share, layout, tiles, first, added, ends, last, len(ready)),
        out_shape=out_shape,
        in_specs=in_specs,
        out_specs=[whole] * len(out_shape),
        scratch_shapes=scratch,
        compiler_params=pltpu.CompilerParams(vmem_limit_bytes=VMEM_LIMIT),
        cost_estimate=pl.CostEstimate(
            flops=cells * depth * 18, bytes_accessed=4 * cells + 8 * cols * depth, transcendentals=3 * cells
        ),
        name="half_grads",
    )(*args)


def local(groups, col_groups, cooc, tile_list, marginal, embed, accum):
    assert col_groups == 2 * groups and groups & (groups - 1) == 0
    both = ("row", "col")
    g = lax.axis_index("row")
    h = lax.axis_index("col")
    chip = h // 2
    core = h % 2
    share, depth = embed.shape
    half = share // 2
    quarter = share // 4
    rows = range(groups)

    def ident(row, at, core):
        return row * col_groups + at * 2 + core

    def permute(value, pairs):
        return lax.ppermute(value, both, pairs)

    def swapped(value, axis, m):
        return lax.ppermute(value, axis, [(r, r ^ m) for r in range(lax.axis_size(axis))])

    def row_swapped(value, m):
        return swapped(value, "row", m)

    def across(value):
        return swapped(value, "col", 1)

    marg_f = marginal.astype(jnp.float32)
    logs = jnp.log(marg_f)

    plane_total = jnp.broadcast_to(jnp.sum(marg_f), (8, 128))
    step = 1
    while step < groups:
        plane_total = plane_total + row_swapped(plane_total, step)
        step *= 2

    def to_line(k):
        came = []
        for c in (0, 1):
            at = k * half + c * quarter
            under = jnp.pad(logs[at : at + quarter].reshape(1, quarter), ((0, PAD - 1), (0, depth - quarter)))
            part = jnp.concatenate([embed[at : at + quarter], under], axis=0)
            came.append(permute(part, [(ident(r, q // 2, q % 2), ident(q, r, c)) for q in rows for r in rows]))
        return jnp.where(core == 0, came[0], came[1])

    def along_line(part, after=()):
        step = groups // 2
        while step > 1:
            came = swapped(part, "col", 2 * step)
            part = part[: part.shape[0] - 2 * len(after)]
            part = jnp.concatenate([part, *[array[:2] for array in after], came], axis=0)
            after = ()
            step //= 2
        return part, swapped(part, "col", 2)

    under = jnp.pad(logs.reshape(share // depth, depth), ((0, PAD - share // depth), (0, 0)))
    coded = jnp.concatenate([embed, under], axis=0)
    pieces = {0: [coded]}
    layout = [(0, 0, share + PAD)]
    for m in range(1, groups):
        if m & (m - 1) == 0 or groups != 4:
            pieces[m] = [row_swapped(coded, m)]
            layout.append((m, 0, share + PAD))
    if groups == 4:
        pieces[3] = [row_swapped(pieces[2][0][:half], 1), row_swapped(pieces[1][0][half:], 2)]
        layout += [(3, 0, half), (3, half, half + PAD)]
    held = [pieces[m][start > 0] for m, start, _ in layout]

    part = to_line(0)
    part_row = lax.broadcasted_iota(jnp.int32, part.shape, 0)
    part = jnp.where(part_row == quarter + 1, plane_total[0, 0], part)
    for number, m in enumerate([1 << q for q in range(groups.bit_length() - 1)]):
        part = jnp.where(part_row == quarter + 2 + number, pieces[m][0][: quarter + PAD], part)
    lower, upper = along_line(part, pieces[3] if groups == 4 else ())
    vectors = [lower, upper, across(lower), across(upper)]

    listing = tile_list.reshape(-1)
    listed = jnp.sum((listing[None, :] == jnp.arange(listing.shape[0])[:, None]).astype(jnp.int32), axis=1)
    place = jnp.stack([g, chip, core]).astype(jnp.int32)

    def from_line_at_once(outs):
        summed = outs[0] + across(outs[1])
        parts = {d: summed[j * quarter : (j + 1) * quarter] for j, d in enumerate(order_of(groups))}
        total = parts[0]
        for d in range(1, groups):
            total = total + swapped(parts[d], "col", 2 * d)
        return summed, total

    def from_line(outs):
        total = outs[0] + across(outs[1])
        step = 1
        while step < groups:
            kept = total.shape[0] // 2
            came = swapped(total[kept:], "col", 2 * step)
            first_came = came if step == 1 else first_came
            total = total[:kept] + came
            step *= 2
        return first_came, total

    def to_home(total):
        homes = []
        for c in (0, 1):
            homes.append(permute(total, [(ident(q, r, c), ident(r, q // 2, q % 2)) for q in rows for r in rows]))
        return homes

    tiles = [(row, col) for row in range(groups * share // BLOCK) for col in range(groups * share // BLOCK)]
    grads = functools.partial(half_grads, groups=groups, share=share, layout=layout, place=place, listed=listed, cooc=cooc)
    lower, upper = along_line(to_line(1))
    outs = grads(0, tiles=tiles[:-1], vectors=vectors, held=held, row_in=None, ready=[lower])
    columns = outs[1:4]
    outs = grads(0, tiles=tiles[-1:], vectors=vectors, held=outs[1:], row_in=outs[0], ready=[upper])
    first_summed, first_total = from_line_at_once(outs)
    vectors = [lower, upper, across(lower), across(upper)]
    outs = grads(1, tiles=tiles[:-1], vectors=vectors, held=[*columns, outs[2]], row_in=None, ready=[first_summed])
    outs = grads(1, tiles=tiles[-1:], vectors=vectors, held=[*columns, outs[1]], row_in=outs[0], ready=[first_total])
    second_came, second_total = from_line(outs)
    first_quarters = to_home(first_total)
    quarters = first_quarters + to_home(second_total)

    halves = outs[2:]
    if groups == 4:
        spare = second_came[:PAD] + first_quarters[0][:PAD] + first_quarters[1][:PAD]
        first_x = row_swapped(jnp.concatenate([halves[2], halves[6], spare], axis=0), 1)[: 2 * half]
        first_y = row_swapped(jnp.concatenate([halves[5], halves[7], spare], axis=0), 2)[: 2 * half]
        second_x = row_swapped(halves[3] + first_y[half:], 1)
        second_y = row_swapped(halves[4] + first_x[half:], 2)
        top = halves[0] + first_x[:half] + second_y
        bottom = halves[1] + second_x + first_y[:half]
    else:
        top, bottom = halves[:2]
        for m in range(1, groups):
            top = top + row_swapped(halves[2 * m], m)
            bottom = bottom + row_swapped(halves[2 * m + 1], m)
    gradients = (jnp.concatenate([top, bottom], axis=0) + jnp.concatenate(quarters, axis=0)) / BLOCK
    new_accum = accum + gradients * gradients
    new_embed = embed - LEARN_RATE * gradients / jnp.sqrt(new_accum)
    return (new_embed, new_accum)


def solution(mesh):
    placed = (
        P("row", "col"),
        P("row", "col", None),
        P(("col", "row")),
        P(("col", "row"), None),
        P(("col", "row"), None),
    )
    return jax.shard_map(
        functools.partial(local, mesh.shape["row"], mesh.shape["col"]),
        mesh=mesh,
        in_specs=placed,
        out_specs=(P(("col", "row"), None), P(("col", "row"), None)),
        check_vma=False,
    )
```

```python
import functools

import jax
import jax.numpy as jnp
from jax import lax
from jax.experimental import pallas as pl
from jax.experimental.pallas import tpu as pltpu
from jax.sharding import PartitionSpec as P

BLOCK = 1024
LEARN_RATE = 0.05
SUB = 512
PAD = 8
VMEM_LIMIT = 42 * 2**20


def split_bf16(values):
    high = values.astype(jnp.bfloat16)
    low = (values - high.astype(jnp.float32)).astype(jnp.bfloat16)
    return high, low


def product(left, right, dims):
    (left_at,), (right_at,) = dims
    left = jnp.concatenate([left[0], left[1], left[0]], axis=left_at)
    right = jnp.concatenate([right[0], right[0], right[1]], axis=right_at)
    return lax.dot_general(left, right, (dims, ((), ())), preferred_element_type=jnp.float32)


def order_of(count):
    order = [0]
    step = count // 2
    while step:
        order += [d + step for d in order]
        step //= 2
    return order


def half_kernel(k, groups, share, layout, tiles, first, added, ends, last, extra, *refs):
    rest = list(refs)
    take = lambda count: [rest.pop(0) for _ in range(count)]
    place_ref, listed_ref, cooc_ref = take(3)
    row_refs = take(4)
    order = order_of(groups)
    if first:
        pieces = take(len(layout))
    else:
        high_ref, low_ref, log_ref, sums_in = take(4)
    if added:
        (row_in,) = take(1)
    take(extra)
    if ends:
        mine_out, other_out = take(2)
    else:
        (row_out,) = take(1)
    if first:
        high_ref, low_ref, log_ref = take(3)
    if last:
        outs = take(2 * groups)
    else:
        (sums,) = take(1)
    row_vecs, row_logs, cells, cell_sems = take(4)
    if ends:
        (row_out,) = take(1)
    if last:
        (sums,) = take(1)

    depth = row_vecs.shape[1]
    half = share // 2
    quarter = share // 4
    cols = groups * share
    col_blocks = cols // BLOCK
    per = BLOCK // share
    tall = BLOCK // 2
    g = place_ref[0]
    chip = place_ref[1]
    core = place_ref[2]

    def cell_copies(row, col):
        number = tiles.index((row, col))
        return [
            pltpu.make_async_copy(
                cooc_ref.at[pl.ds((row * per + j) * share + k * half, half), pl.ds(col * BLOCK, BLOCK)],
                cells.at[number, pl.ds(j * half, half), :],
                cell_sems.at[number, j],
            )
            for j in range(per)
        ]

    for row, col in tiles:

        @pl.when(listed_ref[row * col_blocks + col] > 0)
        def _():
            for copy in cell_copies(row, col):
                copy.start()

    if first:
        total = jnp.zeros((1, 128), jnp.float32)
        for ref in row_refs:
            for j in range(groups // 2):
                at = j * (quarter + PAD) + quarter + 1
                total = total + ref[at : at + 1, :128]
        log_total = jnp.concatenate([jnp.log(total)] * (depth // 128), axis=1)
        for piece, (other, start, count) in zip(pieces, layout):
            body = min(count, share - start)
            at = pl.multiple_of((g ^ other) * share + start, 16)
            high, low = split_bf16(piece[:body, :])
            high_ref[pl.ds(at, body), :] = high
            low_ref[pl.ds(at, body), :] = low
            if body < count:
                at = pl.multiple_of((g ^ other) * PAD, PAD)
                log_ref[pl.ds(at, PAD), :] = piece[body:, :] - log_total
        sums[...] = jnp.zeros_like(sums)
    else:
        sums[...] = sums_in[...]

    for number, ref in enumerate(row_refs):
        side = core if number < 2 else 1 - core
        for j in range(groups // 2):
            d = order[number % 2 * (groups // 2) + j]
            start = j * (quarter + PAD)
            at = pl.multiple_of((chip ^ d) * half + side * quarter, quarter)
            row_vecs[pl.ds(at, quarter), :] = ref[start : start + quarter, :]
            log_row = ref[start + quarter : start + quarter + 1, :128]
            row_logs[pl.ds(at, quarter), :] = jnp.transpose(jnp.broadcast_to(log_row, (128, 128)))[:quarter, :]
    row_out[...] = row_in[...] if added else jnp.zeros_like(row_out)

    for row, col in tiles:
        tall_rows = slice(row * tall, (row + 1) * tall)

        @pl.when(listed_ref[row * col_blocks + col] > 0)
        def _():
            for copy in cell_copies(row, col):
                copy.wait()
            rows = row_vecs[tall_rows, :]
            row_pair = split_bf16(rows)
            row_turned = split_bf16(jnp.transpose(rows))
            row_log = jnp.concatenate([row_logs[tall_rows, :]] * (SUB // 128), axis=1)
            strips = BLOCK // SUB

            def col_pair(strip):
                at = col * BLOCK + strip * SUB
                return high_ref[at : at + SUB, :], low_ref[at : at + SUB, :]

            def scores(strip):
                return product(row_pair, col_pair(strip), ((1,), (1,)))

            def slopes(strip, values):
                at = col * BLOCK + strip * SUB
                log_rows = [lane // share * PAD + lane % share // depth for lane in range(at, at + SUB, depth)]
                col_log = jnp.concatenate([log_ref[q : q + 1, :] for q in log_rows], axis=1)
                centred = values + row_log + col_log
                counts = cells[tiles.index((row, col)), :, strip * SUB : (strip + 1) * SUB]
                counts_f = counts.astype(jnp.float32)
                floor = jnp.maximum(counts_f, 1.0)
                weights = 0.1 + 0.25 * (counts_f * lax.rsqrt(floor))
                return split_bf16(
                    jnp.where(
                        counts_f > 0,
                        weights * (centred - jnp.log(floor)),
                        0.5 * jnp.tanh(0.5 * centred) + 0.5,
                    )
                )

            def gradients(strip, pair):
                at = col * BLOCK + strip * SUB
                row_out[tall_rows, :] += product(pair, col_pair(strip), ((1,), (0,)))
                sums[:, at : at + SUB] += product(row_turned, pair, ((1,), (0,)))

            ahead = scores(0)
            behind = None
            for strip in range(strips):
                values = ahead
                if strip + 1 < strips:
                    ahead = scores(strip + 1)
                if strip > 0:
                    gradients(strip - 1, behind)
                behind = slopes(strip, values)
            gradients(strips - 1, behind)

    for out, side in ((mine_out, core), (other_out, 1 - core)) if ends else ():
        for j, d in enumerate(order):
            at = pl.multiple_of((chip ^ d) * half + side * quarter, quarter)
            out[j * quarter : (j + 1) * quarter, :] = row_out[pl.ds(at, quarter), :]
    if last:
        for other in range(groups):
            at = pl.multiple_of((g ^ other) * share, share)
            block = jnp.transpose(sums[:, pl.ds(at, share)])
            outs[2 * other][...] = block[:half]
            outs[2 * other + 1][...] = block[half:]


def half_grads(k, groups, share, layout, tiles, place, listed, cooc, vectors, held, row_in, ready):
    depth = vectors[0].shape[1]
    cols = groups * share
    first = k == 0 and tiles[0] == (0, 0)
    added = row_in is not None
    ends = tiles[-1] == (cols // BLOCK - 1,) * 2
    last = ends and k == 1
    per = BLOCK // share
    rows = groups * share // 2
    whole = pl.BlockSpec(memory_space=pltpu.VMEM)
    scalar = pl.BlockSpec(memory_space=pltpu.SMEM)
    remote = pl.BlockSpec(memory_space=pl.ANY)
    row_part = jax.ShapeDtypeStruct((rows // 2, depth), jnp.float32)
    row_all = jax.ShapeDtypeStruct((rows, depth), jnp.float32)
    col_half = jax.ShapeDtypeStruct((share // 2, depth), jnp.float32)
    coded = jax.ShapeDtypeStruct((cols, depth), jnp.bfloat16)
    logs = jax.ShapeDtypeStruct((groups * PAD, depth), jnp.float32)
    turned = jax.ShapeDtypeStruct((depth, cols), jnp.float32)
    out_shape = [row_part] * 2 if ends else [row_all]
    out_shape += [coded, coded, logs] if first else []
    out_shape += [col_half] * (2 * groups) if last else [turned]
    held = [*held, row_in] if added else [*held]
    args = [place, listed, cooc, *vectors, *held, *ready]
    in_specs = [scalar] * 2 + [remote] + [whole] * (4 + len(held)) + [remote] * len(ready)
    scratch = [
        pltpu.VMEM((rows, depth), jnp.float32),
        pltpu.VMEM((rows, 128), jnp.float32),
        pltpu.VMEM((len(tiles), BLOCK // 2, BLOCK), jnp.int32),
        pltpu.SemaphoreType.DMA((len(tiles), per)),
    ]
    if ends:
        scratch.append(pltpu.VMEM((rows, depth), jnp.float32))
    if last:
        scratch.append(pltpu.VMEM((depth, cols), jnp.float32))
    cells = len(tiles) * BLOCK * BLOCK // 2
    return pl.pallas_call(
        functools.partial(half_kernel, k, groups, share, layout, tiles, first, added, ends, last, len(ready)),
        out_shape=out_shape,
        in_specs=in_specs,
        out_specs=[whole] * len(out_shape),
        scratch_shapes=scratch,
        compiler_params=pltpu.CompilerParams(vmem_limit_bytes=VMEM_LIMIT),
        cost_estimate=pl.CostEstimate(
            flops=cells * depth * 18, bytes_accessed=4 * cells + 8 * cols * depth, transcendentals=3 * cells
        ),
        name="half_grads",
    )(*args)


def local(groups, col_groups, cooc, tile_list, marginal, embed, accum):
    assert col_groups == 2 * groups and groups & (groups - 1) == 0
    both = ("row", "col")
    g = lax.axis_index("row")
    h = lax.axis_index("col")
    chip = h // 2
    core = h % 2
    share, depth = embed.shape
    half = share // 2
    quarter = share // 4
    rows = range(groups)

    def ident(row, at, core):
        return row * col_groups + at * 2 + core

    def permute(value, pairs):
        return lax.ppermute(value, both, pairs)

    def swapped(value, axis, m):
        return lax.ppermute(value, axis, [(r, r ^ m) for r in range(lax.axis_size(axis))])

    def row_swapped(value, m):
        return swapped(value, "row", m)

    def across(value):
        return swapped(value, "col", 1)

    marg_f = marginal.astype(jnp.float32)
    logs = jnp.log(marg_f)

    plane_total = jnp.broadcast_to(jnp.sum(marg_f), (8, 128))
    step = 1
    while step < groups:
        plane_total = plane_total + row_swapped(plane_total, step)
        step *= 2

    def to_line(k):
        came = []
        for c in (0, 1):
            at = k * half + c * quarter
            under = jnp.pad(logs[at : at + quarter].reshape(1, quarter), ((0, PAD - 1), (0, depth - quarter)))
            part = jnp.concatenate([embed[at : at + quarter], under], axis=0)
            came.append(permute(part, [(ident(r, q // 2, q % 2), ident(q, r, c)) for q in rows for r in rows]))
        return jnp.where(core == 0, came[0], came[1])

    def along_line(part, after=()):
        step = groups // 2
        while step > 1:
            came = swapped(part, "col", 2 * step)
            part = part[: part.shape[0] - 2 * len(after)]
            part = jnp.concatenate([part, *[array[:2] for array in after], came], axis=0)
            after = ()
            step //= 2
        return part, swapped(part, "col", 2)

    under = jnp.pad(logs.reshape(share // depth, depth), ((0, PAD - share // depth), (0, 0)))
    coded = jnp.concatenate([embed, under], axis=0)
    pieces = {0: [coded]}
    layout = [(0, 0, share + PAD)]
    for m in range(1, groups):
        if m & (m - 1) == 0 or groups != 4:
            pieces[m] = [row_swapped(coded, m)]
            layout.append((m, 0, share + PAD))
    if groups == 4:
        pieces[3] = [row_swapped(pieces[2][0][:half], 1), row_swapped(pieces[1][0][half:], 2)]
        layout += [(3, 0, half), (3, half, half + PAD)]
    held = [pieces[m][start > 0] for m, start, _ in layout]

    part = to_line(0)
    part_row = lax.broadcasted_iota(jnp.int32, part.shape, 0)
    part = jnp.where(part_row == quarter + 1, plane_total[0, 0], part)
    for number, m in enumerate([1 << q for q in range(groups.bit_length() - 1)]):
        part = jnp.where(part_row == quarter + 2 + number, pieces[m][0][: quarter + PAD], part)
    lower, upper = along_line(part, pieces[3] if groups == 4 else ())
    vectors = [lower, upper, across(lower), across(upper)]

    listing = tile_list.reshape(-1)
    listed = jnp.sum((listing[None, :] == jnp.arange(listing.shape[0])[:, None]).astype(jnp.int32), axis=1)
    place = jnp.stack([g, chip, core]).astype(jnp.int32)

    def from_line(outs):
        summed = outs[0] + across(outs[1])
        parts = {d: summed[j * quarter : (j + 1) * quarter] for j, d in enumerate(order_of(groups))}
        total = parts[0]
        for d in range(1, groups):
            total = total + swapped(parts[d], "col", 2 * d)
        return summed, total

    def to_home(total):
        homes = []
        for c in (0, 1):
            homes.append(permute(total, [(ident(q, r, c), ident(r, q // 2, q % 2)) for q in rows for r in rows]))
        return homes

    tiles = [(row, col) for row in range(groups * share // BLOCK) for col in range(groups * share // BLOCK)]
    grads = functools.partial(half_grads, groups=groups, share=share, layout=layout, place=place, listed=listed, cooc=cooc)
    lower, upper = along_line(to_line(1))
    outs = grads(0, tiles=tiles[:-1], vectors=vectors, held=held, row_in=None, ready=[lower])
    columns = outs[1:4]
    outs = grads(0, tiles=tiles[-1:], vectors=vectors, held=outs[1:], row_in=outs[0], ready=[upper])
    first_summed, first_total = from_line(outs)
    vectors = [lower, upper, across(lower), across(upper)]
    outs = grads(1, tiles=tiles[:-1], vectors=vectors, held=[*columns, outs[2]], row_in=None, ready=[first_summed])
    outs = grads(1, tiles=tiles[-1:], vectors=vectors, held=[*columns, outs[1]], row_in=outs[0], ready=[first_total])
    second_summed, second_total = from_line(outs)
    first_quarters = to_home(first_total)
    quarters = first_quarters + to_home(second_total)

    halves = outs[2:]
    if groups == 4:
        spare = second_summed[:PAD] + first_quarters[0][:PAD] + first_quarters[1][:PAD]
        first_x = row_swapped(jnp.concatenate([halves[2], halves[6], spare], axis=0), 1)[: 2 * half]
        first_y = row_swapped(jnp.concatenate([halves[5], halves[7], spare], axis=0), 2)[: 2 * half]
        second_x = row_swapped(halves[3] + first_y[half:], 1)
        second_y = row_swapped(halves[4] + first_x[half:], 2)
        top = halves[0] + first_x[:half] + second_y
        bottom = halves[1] + second_x + first_y[:half]
    else:
        top, bottom = halves[:2]
        for m in range(1, groups):
            top = top + row_swapped(halves[2 * m], m)
            bottom = bottom + row_swapped(halves[2 * m + 1], m)
    gradients = (jnp.concatenate([top, bottom], axis=0) + jnp.concatenate(quarters, axis=0)) / BLOCK
    new_accum = accum + gradients * gradients
    new_embed = embed - LEARN_RATE * gradients / jnp.sqrt(new_accum)
    return (new_embed, new_accum)


def solution(mesh):
    placed = (
        P("row", "col"),
        P("row", "col", None),
        P(("col", "row")),
        P(("col", "row"), None),
        P(("col", "row"), None),
    )
    return jax.shard_map(
        functools.partial(local, mesh.shape["row"], mesh.shape["col"]),
        mesh=mesh,
        in_specs=placed,
        out_specs=(P(("col", "row"), None), P(("col", "row"), None)),
        check_vma=False,
    )
```

```python
import functools

import jax
import jax.numpy as jnp
from jax import lax
from jax.experimental import pallas as pl
from jax.experimental.pallas import tpu as pltpu
from jax.sharding import PartitionSpec as P

BLOCK = 1024
LEARN_RATE = 0.05
SUB = 1024
PAD = 8
VMEM_LIMIT = 42 * 2**20


def split_bf16(values):
    high = values.astype(jnp.bfloat16)
    low = (values - high.astype(jnp.float32)).astype(jnp.bfloat16)
    return high, low


def product(left, right, dims):
    (left_at,), (right_at,) = dims
    left = jnp.concatenate([left[0], left[1], left[0]], axis=left_at)
    right = jnp.concatenate([right[0], right[0], right[1]], axis=right_at)
    return lax.dot_general(left, right, (dims, ((), ())), preferred_element_type=jnp.float32)


def order_of(count):
    order = [0]
    step = count // 2
    while step:
        order += [d + step for d in order]
        step //= 2
    return order


def half_kernel(k, groups, share, layout, tiles, first, added, ends, last, extra, *refs):
    rest = list(refs)
    take = lambda count: [rest.pop(0) for _ in range(count)]
    place_ref, listed_ref, cooc_ref = take(3)
    row_refs = take(4)
    order = order_of(groups)
    if first:
        pieces = take(len(layout))
    else:
        high_ref, low_ref, log_ref, sums_in = take(4)
    if added:
        (row_in,) = take(1)
    take(extra)
    if ends:
        mine_out, other_out = take(2)
    else:
        (row_out,) = take(1)
    if first:
        high_ref, low_ref, log_ref = take(3)
    if last:
        outs = take(2 * groups)
    else:
        (sums,) = take(1)
    row_vecs, row_logs, cells, cell_sems = take(4)
    if ends:
        (row_out,) = take(1)
    if last:
        (sums,) = take(1)

    depth = row_vecs.shape[1]
    half = share // 2
    quarter = share // 4
    cols = groups * share
    col_blocks = cols // BLOCK
    per = BLOCK // share
    tall = BLOCK // 2
    g = place_ref[0]
    chip = place_ref[1]
    core = place_ref[2]

    def cell_copies(row, col):
        number = tiles.index((row, col))
        return [
            pltpu.make_async_copy(
                cooc_ref.at[pl.ds((row * per + j) * share + k * half, half), pl.ds(col * BLOCK, BLOCK)],
                cells.at[number, pl.ds(j * half, half), :],
                cell_sems.at[number, j],
            )
            for j in range(per)
        ]

    for row, col in tiles:

        @pl.when(listed_ref[row * col_blocks + col] > 0)
        def _():
            for copy in cell_copies(row, col):
                copy.start()

    if first:
        total = jnp.zeros((1, 128), jnp.float32)
        for ref in row_refs:
            for j in range(groups // 2):
                at = j * (quarter + PAD) + quarter + 1
                total = total + ref[at : at + 1, :128]
        log_total = jnp.concatenate([jnp.log(total)] * (depth // 128), axis=1)
        for piece, (other, start, count) in zip(pieces, layout):
            body = min(count, share - start)
            at = pl.multiple_of((g ^ other) * share + start, 16)
            high, low = split_bf16(piece[:body, :])
            high_ref[pl.ds(at, body), :] = high
            low_ref[pl.ds(at, body), :] = low
            if body < count:
                at = pl.multiple_of((g ^ other) * PAD, PAD)
                log_ref[pl.ds(at, PAD), :] = piece[body:, :] - log_total
        sums[...] = jnp.zeros_like(sums)
    else:
        sums[...] = sums_in[...]

    for number, ref in enumerate(row_refs):
        side = core if number < 2 else 1 - core
        for j in range(groups // 2):
            d = order[number % 2 * (groups // 2) + j]
            start = j * (quarter + PAD)
            at = pl.multiple_of((chip ^ d) * half + side * quarter, quarter)
            row_vecs[pl.ds(at, quarter), :] = ref[start : start + quarter, :]
            log_row = ref[start + quarter : start + quarter + 1, :128]
            row_logs[pl.ds(at, quarter), :] = jnp.transpose(jnp.broadcast_to(log_row, (128, 128)))[:quarter, :]
    row_out[...] = row_in[...] if added else jnp.zeros_like(row_out)

    for row, col in tiles:
        tall_rows = slice(row * tall, (row + 1) * tall)

        @pl.when(listed_ref[row * col_blocks + col] > 0)
        def _():
            for copy in cell_copies(row, col):
                copy.wait()
            rows = row_vecs[tall_rows, :]
            row_pair = split_bf16(rows)
            row_turned = split_bf16(jnp.transpose(rows))
            row_log = jnp.concatenate([row_logs[tall_rows, :]] * (SUB // 128), axis=1)
            strips = BLOCK // SUB

            def col_pair(strip):
                at = col * BLOCK + strip * SUB
                return high_ref[at : at + SUB, :], low_ref[at : at + SUB, :]

            def scores(strip):
                return product(row_pair, col_pair(strip), ((1,), (1,)))

            def slopes(strip, values):
                at = col * BLOCK + strip * SUB
                log_rows = [lane // share * PAD + lane % share // depth for lane in range(at, at + SUB, depth)]
                col_log = jnp.concatenate([log_ref[q : q + 1, :] for q in log_rows], axis=1)
                centred = values + row_log + col_log
                counts = cells[tiles.index((row, col)), :, strip * SUB : (strip + 1) * SUB]
                counts_f = counts.astype(jnp.float32)
                floor = jnp.maximum(counts_f, 1.0)
                weights = 0.1 + 0.25 * (counts_f * lax.rsqrt(floor))
                return split_bf16(
                    jnp.where(
                        counts_f > 0,
                        weights * (centred - jnp.log(floor)),
                        0.5 * jnp.tanh(0.5 * centred) + 0.5,
                    )
                )

            def gradients(strip, pair):
                at = col * BLOCK + strip * SUB
                row_out[tall_rows, :] += product(pair, col_pair(strip), ((1,), (0,)))
                sums[:, at : at + SUB] += product(row_turned, pair, ((1,), (0,)))

            ahead = scores(0)
            behind = None
            for strip in range(strips):
                values = ahead
                if strip + 1 < strips:
                    ahead = scores(strip + 1)
                if strip > 0:
                    gradients(strip - 1, behind)
                behind = slopes(strip, values)
            gradients(strips - 1, behind)

    for out, side in ((mine_out, core), (other_out, 1 - core)) if ends else ():
        for j, d in enumerate(order):
            at = pl.multiple_of((chip ^ d) * half + side * quarter, quarter)
            out[j * quarter : (j + 1) * quarter, :] = row_out[pl.ds(at, quarter), :]
    if last:
        for other in range(groups):
            at = pl.multiple_of((g ^ other) * share, share)
            block = jnp.transpose(sums[:, pl.ds(at, share)])
            outs[2 * other][...] = block[:half]
            outs[2 * other + 1][...] = block[half:]


def half_grads(k, groups, share, layout, tiles, place, listed, cooc, vectors, held, row_in, ready):
    depth = vectors[0].shape[1]
    cols = groups * share
    first = k == 0 and tiles[0] == (0, 0)
    added = row_in is not None
    ends = tiles[-1] == (cols // BLOCK - 1,) * 2
    last = ends and k == 1
    per = BLOCK // share
    rows = groups * share // 2
    whole = pl.BlockSpec(memory_space=pltpu.VMEM)
    scalar = pl.BlockSpec(memory_space=pltpu.SMEM)
    remote = pl.BlockSpec(memory_space=pl.ANY)
    row_part = jax.ShapeDtypeStruct((rows // 2, depth), jnp.float32)
    row_all = jax.ShapeDtypeStruct((rows, depth), jnp.float32)
    col_half = jax.ShapeDtypeStruct((share // 2, depth), jnp.float32)
    coded = jax.ShapeDtypeStruct((cols, depth), jnp.bfloat16)
    logs = jax.ShapeDtypeStruct((groups * PAD, depth), jnp.float32)
    turned = jax.ShapeDtypeStruct((depth, cols), jnp.float32)
    out_shape = [row_part] * 2 if ends else [row_all]
    out_shape += [coded, coded, logs] if first else []
    out_shape += [col_half] * (2 * groups) if last else [turned]
    held = [*held, row_in] if added else [*held]
    args = [place, listed, cooc, *vectors, *held, *ready]
    in_specs = [scalar] * 2 + [remote] + [whole] * (4 + len(held)) + [remote] * len(ready)
    scratch = [
        pltpu.VMEM((rows, depth), jnp.float32),
        pltpu.VMEM((rows, 128), jnp.float32),
        pltpu.VMEM((len(tiles), BLOCK // 2, BLOCK), jnp.int32),
        pltpu.SemaphoreType.DMA((len(tiles), per)),
    ]
    if ends:
        scratch.append(pltpu.VMEM((rows, depth), jnp.float32))
    if last:
        scratch.append(pltpu.VMEM((depth, cols), jnp.float32))
    cells = len(tiles) * BLOCK * BLOCK // 2
    return pl.pallas_call(
        functools.partial(half_kernel, k, groups, share, layout, tiles, first, added, ends, last, len(ready)),
        out_shape=out_shape,
        in_specs=in_specs,
        out_specs=[whole] * len(out_shape),
        scratch_shapes=scratch,
        compiler_params=pltpu.CompilerParams(vmem_limit_bytes=VMEM_LIMIT),
        cost_estimate=pl.CostEstimate(
            flops=cells * depth * 18, bytes_accessed=4 * cells + 8 * cols * depth, transcendentals=3 * cells
        ),
        name="half_grads",
    )(*args)


def local(groups, col_groups, cooc, tile_list, marginal, embed, accum):
    assert col_groups == 2 * groups and groups & (groups - 1) == 0
    both = ("row", "col")
    g = lax.axis_index("row")
    h = lax.axis_index("col")
    chip = h // 2
    core = h % 2
    share, depth = embed.shape
    half = share // 2
    quarter = share // 4
    rows = range(groups)

    def ident(row, at, core):
        return row * col_groups + at * 2 + core

    def permute(value, pairs):
        return lax.ppermute(value, both, pairs)

    def swapped(value, axis, m):
        return lax.ppermute(value, axis, [(r, r ^ m) for r in range(lax.axis_size(axis))])

    def row_swapped(value, m):
        return swapped(value, "row", m)

    def across(value):
        return swapped(value, "col", 1)

    marg_f = marginal.astype(jnp.float32)
    logs = jnp.log(marg_f)

    plane_total = jnp.broadcast_to(jnp.sum(marg_f), (8, 128))
    step = 1
    while step < groups:
        plane_total = plane_total + row_swapped(plane_total, step)
        step *= 2

    def to_line(k):
        came = []
        for c in (0, 1):
            at = k * half + c * quarter
            under = jnp.pad(logs[at : at + quarter].reshape(1, quarter), ((0, PAD - 1), (0, depth - quarter)))
            part = jnp.concatenate([embed[at : at + quarter], under], axis=0)
            came.append(permute(part, [(ident(r, q // 2, q % 2), ident(q, r, c)) for q in rows for r in rows]))
        return jnp.where(core == 0, came[0], came[1])

    def along_line(part, after=()):
        step = groups // 2
        while step > 1:
            came = swapped(part, "col", 2 * step)
            part = part[: part.shape[0] - 2 * len(after)]
            part = jnp.concatenate([part, *[array[:2] for array in after], came], axis=0)
            after = ()
            step //= 2
        return part, swapped(part, "col", 2)

    under = jnp.pad(logs.reshape(share // depth, depth), ((0, PAD - share // depth), (0, 0)))
    coded = jnp.concatenate([embed, under], axis=0)
    pieces = {0: [coded]}
    layout = [(0, 0, share + PAD)]
    for m in range(1, groups):
        if m & (m - 1) == 0 or groups != 4:
            pieces[m] = [row_swapped(coded, m)]
            layout.append((m, 0, share + PAD))
    if groups == 4:
        pieces[3] = [row_swapped(pieces[2][0][:half], 1), row_swapped(pieces[1][0][half:], 2)]
        layout += [(3, 0, half), (3, half, half + PAD)]
    held = [pieces[m][start > 0] for m, start, _ in layout]

    part = to_line(0)
    part_row = lax.broadcasted_iota(jnp.int32, part.shape, 0)
    part = jnp.where(part_row == quarter + 1, plane_total[0, 0], part)
    for number, m in enumerate([1 << q for q in range(groups.bit_length() - 1)]):
        part = jnp.where(part_row == quarter + 2 + number, pieces[m][0][: quarter + PAD], part)
    lower, upper = along_line(part, pieces[3] if groups == 4 else ())
    vectors = [lower, upper, across(lower), across(upper)]

    listing = tile_list.reshape(-1)
    listed = jnp.sum((listing[None, :] == jnp.arange(listing.shape[0])[:, None]).astype(jnp.int32), axis=1)
    place = jnp.stack([g, chip, core]).astype(jnp.int32)

    def from_line(outs):
        summed = outs[0] + across(outs[1])
        parts = {d: summed[j * quarter : (j + 1) * quarter] for j, d in enumerate(order_of(groups))}
        total = parts[0]
        for d in range(1, groups):
            total = total + swapped(parts[d], "col", 2 * d)
        return summed, total

    def to_home(total):
        homes = []
        for c in (0, 1):
            homes.append(permute(total, [(ident(q, r, c), ident(r, q // 2, q % 2)) for q in rows for r in rows]))
        return homes

    tiles = [(row, col) for row in range(groups * share // BLOCK) for col in range(groups * share // BLOCK)]
    grads = functools.partial(half_grads, groups=groups, share=share, layout=layout, place=place, listed=listed, cooc=cooc)
    lower, upper = along_line(to_line(1))
    outs = grads(0, tiles=tiles[:-1], vectors=vectors, held=held, row_in=None, ready=[lower])
    columns = outs[1:4]
    outs = grads(0, tiles=tiles[-1:], vectors=vectors, held=outs[1:], row_in=outs[0], ready=[upper])
    first_summed, first_total = from_line(outs)
    vectors = [lower, upper, across(lower), across(upper)]
    outs = grads(1, tiles=tiles[:-1], vectors=vectors, held=[*columns, outs[2]], row_in=None, ready=[first_summed])
    outs = grads(1, tiles=tiles[-1:], vectors=vectors, held=[*columns, outs[1]], row_in=outs[0], ready=[first_total])
    second_summed, second_total = from_line(outs)
    first_quarters = to_home(first_total)
    quarters = first_quarters + to_home(second_total)

    halves = outs[2:]
    if groups == 4:
        spare = second_summed[:PAD] + first_quarters[0][:PAD] + first_quarters[1][:PAD]
        first_x = row_swapped(jnp.concatenate([halves[2], halves[6], spare], axis=0), 1)[: 2 * half]
        first_y = row_swapped(jnp.concatenate([halves[5], halves[7], spare], axis=0), 2)[: 2 * half]
        second_x = row_swapped(halves[3] + first_y[half:], 1)
        second_y = row_swapped(halves[4] + first_x[half:], 2)
        top = halves[0] + first_x[:half] + second_y
        bottom = halves[1] + second_x + first_y[:half]
    else:
        top, bottom = halves[:2]
        for m in range(1, groups):
            top = top + row_swapped(halves[2 * m], m)
            bottom = bottom + row_swapped(halves[2 * m + 1], m)
    gradients = (jnp.concatenate([top, bottom], axis=0) + jnp.concatenate(quarters, axis=0)) / BLOCK
    new_accum = accum + gradients * gradients
    new_embed = embed - LEARN_RATE * gradients / jnp.sqrt(new_accum)
    return (new_embed, new_accum)


def solution(mesh):
    placed = (
        P("row", "col"),
        P("row", "col", None),
        P(("col", "row")),
        P(("col", "row"), None),
        P(("col", "row"), None),
    )
    return jax.shard_map(
        functools.partial(local, mesh.shape["row"], mesh.shape["col"]),
        mesh=mesh,
        in_specs=placed,
        out_specs=(P(("col", "row"), None), P(("col", "row"), None)),
        check_vma=False,
    )
```
